512 devices in a mesh: gx: 16 (over z_lo, y), gy: 32 (over x, z_hi, core).
Axes of the slice: x: 4, y: 8, z: 8 (z_hi: 4, z_lo: 2; z = z_hi * 2 + z_lo), core: 2. Of those that a mesh axis runs over, the one named last changes fastest.
Arguments:
- displacement: bfloat16 [3, 16, 256, 2048], P(None, None, 'gy', 'gx'), may hold values from -6 to 6
- density: float32 [16, 256, 2048], P(None, 'gy', 'gx'), may hold values from 0.3 to 1
- solid: int32 [16, 256, 2048], P(None, 'gy', 'gx'), may hold values 0 or 1
- fixed_nodes: int32 [4096], replicated, may hold values from 0 to 8388607
- load_nodes: int32 [512], replicated, may hold values from 0 to 8388607
- load_forces: float32 [512, 3], replicated, may hold values from -6 to 6
Outputs:
- smoothed: bfloat16 [3, 16, 256, 2048], P(None, None, 'gy', 'gx')
- filtered: float32 [16, 256, 2048], P(None, 'gy', 'gx')
The draws below stay inside these ranges and needn't reach their ends.
Inputs may be any that keep to these rules, and one draw needn't show every extreme that they name: `fixed_nodes`: global node indices; a node may appear more than once. `load_nodes`: global node indices; forces at a repeated node add up.
All inputs are finite; a program needn't handle non-finite values. No bound on the sum of `solid` on one device may be relied on, other than what follows from the above.
Results may differ from the reference program's by a relative error of at most 0.0092.
Values may be sent and summed in bfloat16 or wider, within the bound.
No kernel may reach another device: no remote copies, remote signals or barrier semaphores. Data moves between devices by JAX's collectives and lax.ppermute only.
A program may use at most 64 MiB of HBM per device.

```python
import math
import jax
import jax.numpy as jnp
import numpy as np
from jax import lax

CY = 8
DEPTH = 16
FIXED = 4096
LOADS = 512
NX = 2048
NY = 256
N_GY = 32


def touch_ends(entries, key, low, top_value):
    shape = entries.shape
    index_at = [jax.random.randint(jax.random.fold_in(key, axis), (), 0, shape[axis]) for axis in range(len(shape))]
    entries = entries.at[tuple(index_at)].set(low)
    longest = shape.index(max(shape))
    index_at[longest] = (index_at[longest] + 1) % shape[longest]
    return entries.at[tuple(index_at)].set(top_value)


def steps_of(rng, shape, pieces, least, largest):
    def one(position, blocks):
        draws = jax.random.uniform(jax.random.fold_in(jax.random.fold_in(rng, 6), position), (blocks,), jnp.float32, least / len(pieces), largest / len(pieces))
        return jnp.repeat(jnp.exp(draws), shape[position] // blocks).reshape((-1,) + (1,) * (len(shape) - position - 1))

    level = one(*pieces[0])
    for cut in pieces[1:]:
        level = level * one(*cut)
    return level


def scatter_about(key, shape, width, bound, shards=(), held_as=jnp.bfloat16):
    level = steps_of(key, shape, shards, -0.22, 0.18) if shards else 1.0
    array = jax.random.normal(key, shape, jnp.float32) * width * level
    return jnp.minimum(jnp.maximum(array, -bound), bound).astype(held_as)


def setup_inputs(seed: int = 0) -> dict:
    streams_of = jax.random.split(jax.random.key(seed), 7)
    return {
        "displacement": scatter_about(streams_of[0], (3, DEPTH, NY, NX), 1.0, 6.0, ((2, 32), (3, 16))),
        "density": jnp.clip(jnp.exp(math.log(1.0) - 1.2039728 * jax.random.uniform(streams_of[1], (DEPTH, NY, NX), jnp.float32) ** steps_of(streams_of[1], (DEPTH, NY, NX), ((1, 32), (2, 16)), -0.2, 0.2)), 0.3, 1.0),
        "solid": touch_ends((jax.random.randint(streams_of[2], (DEPTH, NY, NX), 0, 8) < 1).astype(jnp.int32), jax.random.fold_in(streams_of[2], 1), 0, 1),
        "fixed_nodes": touch_ends(jax.random.randint(streams_of[3], (FIXED,), 0, NX * NY * DEPTH), jax.random.fold_in(streams_of[3], 1), 0, (NX * NY * DEPTH) - 1).astype(jnp.int32),
        "load_nodes": touch_ends(jax.random.randint(streams_of[4], (LOADS,), 0, NX * NY * DEPTH), jax.random.fold_in(streams_of[4], 1), 0, (NX * NY * DEPTH) - 1).astype(jnp.int32),
        "load_forces": scatter_about(streams_of[5], (LOADS, 3), 1.0, 6.0, (), jnp.float32),
    }


void_modulus = 0.001
spectral_mid = 1.375
spectral_half = 1.125

def stiffness_table():
    poisson = 0.3
    lame = poisson / ((1.0 + poisson) * (1.0 - 2.0 * poisson))
    shear = 0.5 / (1.0 + poisson)
    elastic = np.zeros((6, 6))
    elastic[:3, :3] = lame
    for index in range(3):
        elastic[index, index] += 2.0 * shear
        elastic[index + 3, index + 3] = shear
    points = [0.5 - 0.5 / math.sqrt(3.0), 0.5 + 0.5 / math.sqrt(3.0)]
    table = np.zeros((24, 24))
    for point_z in points:
        for point_y in points:
            for point_x in points:
                strain = np.zeros((6, 24))
                for corner in range(8):
                    bit_z, bit_y, bit_x = (corner // 4, corner // 2 % 2, corner % 2)
                    shape_x = point_x if bit_x else 1.0 - point_x
                    shape_y = point_y if bit_y else 1.0 - point_y
                    shape_z = point_z if bit_z else 1.0 - point_z
                    slope_x = 1.0 if bit_x else -1.0
                    slope_y = 1.0 if bit_y else -1.0
                    slope_z = 1.0 if bit_z else -1.0
                    grad_x = slope_x * shape_y * shape_z
                    grad_y = shape_x * slope_y * shape_z
                    grad_z = shape_x * shape_y * slope_z
                    strain[0, corner] = grad_x
                    strain[1, 8 + corner] = grad_y
                    strain[2, 16 + corner] = grad_z
                    strain[3, corner] = grad_y
                    strain[3, 8 + corner] = grad_x
                    strain[4, 8 + corner] = grad_z
                    strain[4, 16 + corner] = grad_y
                    strain[5, corner] = grad_z
                    strain[5, 16 + corner] = grad_x
                table += strain.T @ elastic @ strain / 8.0
    return table

def conic_taps():
    taps = []
    for shift_z in range(-2, 3):
        for shift_y in range(-2, 3):
            for shift_x in range(-2, 3):
                weight = 3.0 - math.sqrt(shift_z * shift_z + shift_y * shift_y + shift_x * shift_x)
                if weight > 0.0:
                    taps.append((shift_z, shift_y, shift_x, weight))
    return taps

def conic_filter(padded, depth, rows, columns):
    total = jnp.zeros((depth, rows, columns), jnp.float32)
    for shift_z, shift_y, shift_x, weight in conic_taps():
        total = total + weight * padded[2 + shift_z:2 + shift_z + depth, 2 + shift_y:2 + shift_y + rows, 2 + shift_x:2 + shift_x + columns]
    return total

def exists_region(z_low, z_count, y_low, rows, x_low, columns):
    zpos = z_low + jnp.arange(z_count, dtype=jnp.int32)
    ypos = y_low + jnp.arange(rows, dtype=jnp.int32)
    xpos = x_low + jnp.arange(columns, dtype=jnp.int32)
    inside_z = ((zpos >= 0) & (zpos < DEPTH - 1))[:, None, None]
    inside_y = ((ypos >= 0) & (ypos < NY - 1))[None, :, None]
    inside_x = ((xpos >= 0) & (xpos < NX - 1))[None, None, :]
    return (inside_z & inside_y & inside_x).astype(jnp.float32)

def element_terms(upper, table, rows, columns):
    padded = jnp.pad(upper, ((0, 0), (0, 1), (0, 0), (0, 0)))
    stacked = jnp.stack([padded[component, depth_bit:depth_bit + DEPTH, row_bit:row_bit + rows, col_bit:col_bit + columns] for component in range(3) for depth_bit in (0, 1) for row_bit in (0, 1) for col_bit in (0, 1)])
    stacked = stacked.astype(jnp.float32)
    product = jnp.tensordot(table, stacked, axes=1, precision=lax.Precision.HIGHEST)
    return (stacked, product)

def group_depth(terms, rows, columns):
    count = terms.shape[0] // 8
    split = terms.reshape(count, 2, 2, 2, DEPTH, rows, columns)
    high = split[:, 1]
    moved = jnp.concatenate([jnp.zeros_like(high[:, :, :, :1]), high[:, :, :, :-1]], axis=3)
    return split[:, 0] + moved

def gather_corners(grouped, rows, columns):
    total = grouped[:, 0, 0, :, 1:1 + rows, 1:1 + columns]
    total = total + grouped[:, 0, 1, :, 1:1 + rows, 0:columns]
    total = total + grouped[:, 1, 0, :, 0:rows, 1:1 + columns]
    total = total + grouped[:, 1, 1, :, 0:rows, 0:columns]
    return total

def operate(field, stiffness, table, diag_terms, with_diag):
    node_pad = jnp.pad(field, ((0, 0), (0, 0), (1, 1), (1, 1)))
    stiff_pad = jnp.pad(stiffness, ((0, 0), (1, 0), (1, 0)))
    zero = jnp.zeros((), jnp.int32)

    def block(index):
        start = (index * CY).astype(jnp.int32)
        nodes = lax.dynamic_slice(node_pad, (zero, zero, start, zero), (3, DEPTH, CY + 2, NX + 2))
        stiff_block = lax.dynamic_slice(stiff_pad, (zero, start, zero), (DEPTH, CY + 1, NX + 1))
        stacked, product = element_terms(nodes, table, CY + 1, NX + 1)
        terms = product * stiff_block
        if with_diag:
            terms = jnp.concatenate([terms, diag_terms[:, None, None, None] * stiff_block], axis=0)
        return gather_corners(group_depth(terms, CY + 1, NX + 1), CY, NX)
    blocks = lax.map(block, jnp.arange(N_GY, dtype=jnp.int32))
    count = blocks.shape[1]
    return jnp.transpose(blocks, (1, 2, 0, 3, 4)).reshape(count, DEPTH, NY, NX)

def energy_field(field, table):
    node_pad = jnp.pad(field, ((0, 0), (0, 0), (0, 1), (0, 1)))
    zero = jnp.zeros((), jnp.int32)

    def block(index):
        start = (index * CY).astype(jnp.int32)
        nodes = lax.dynamic_slice(node_pad, (zero, zero, start, zero), (3, DEPTH, CY + 1, NX + 1))
        stacked, product = element_terms(nodes, table, CY, NX)
        return lax.optimization_barrier(jnp.sum(stacked * product, axis=0))
    blocks = lax.map(block, jnp.arange(N_GY, dtype=jnp.int32))
    return jnp.transpose(blocks, (1, 0, 2, 3)).reshape(DEPTH, NY, NX)

def reference(displacement, density, solid, fixed_nodes, load_nodes, load_forces):
    table_low = jnp.asarray(stiffness_table(), jnp.float32).astype(jnp.bfloat16)
    table = lax.optimization_barrier(table_low).astype(jnp.float32)
    diag_terms = jnp.diagonal(table)
    exists = exists_region(0, DEPTH, 0, NY, 0, NX)
    designed = (1 - solid).astype(jnp.float32)
    physical = jnp.where(solid == 1, jnp.float32(1.0), density)
    stiffness = (void_modulus + (1.0 - void_modulus) * physical ** 3) * exists
    fixed_x = fixed_nodes % NX
    fixed_y = fixed_nodes // NX % NY
    fixed_z = fixed_nodes // (NX * NY)
    free = jnp.ones((DEPTH, NY, NX), jnp.float32).at[fixed_z, fixed_y, fixed_x].set(0.0)
    load_x = load_nodes % NX
    load_y = load_nodes // NX % NY
    load_z = load_nodes // (NX * NY)
    loads = jnp.zeros((3, DEPTH, NY, NX), jnp.float32).at[:, load_z, load_y, load_x].add(load_forces.T)
    sigma = spectral_mid / spectral_half
    first = 1.0 / sigma
    second = 1.0 / (2.0 * sigma - first)
    both = operate(displacement, stiffness, table, diag_terms, True)
    applied = both[:3]
    diagonal = both[3:]
    residual0 = (loads - applied) * free
    step0 = (residual0 / (spectral_mid * diagonal)).astype(jnp.bfloat16)
    applied1 = operate(step0, stiffness, table, diag_terms, False)
    residual1 = residual0 - applied1 * free
    step1 = second * first * step0.astype(jnp.float32) + 2.0 * second / spectral_half * residual1 / diagonal
    smoothed = (displacement.astype(jnp.float32) + step0.astype(jnp.float32) + step1).astype(jnp.bfloat16)
    energy = energy_field(smoothed, table)
    sensitivity = -3.0 * (1.0 - void_modulus) * physical * physical * exists * designed * energy
    weight_sum = conic_filter(exists_region(-2, DEPTH + 4, -2, NY + 4, -2, NX + 4), DEPTH, NY, NX)
    alive = exists > 0
    ratio = jnp.where(alive, sensitivity / jnp.where(alive, weight_sum, 1.0), 0.0)
    filtered = conic_filter(jnp.pad(ratio, 2), DEPTH, NY, NX) * exists * designed
    return (smoothed, filtered)
```

```python
import math

import jax
import jax.numpy as jnp
import numpy as np
from jax import lax
from jax.experimental import pallas as pl
from jax.experimental.pallas import tpu as pltpu
from jax.sharding import PartitionSpec as P

void_modulus = 0.001
spectral_mid = 1.375
spectral_half = 1.125
sigma = spectral_mid / spectral_half
first = 1.0 / sigma
second = 1.0 / (2.0 * sigma - first)

F32, BF16, I32 = jnp.float32, jnp.bfloat16, jnp.int32
DEPTH, ROWS, COLS = 16, 8, 128
LOW, HIGH = 4, 5
WIDE = 256
SPAN = LOW + HIGH
KLASS = (0, 1, 2, 4, 5, 8)


def stiffness_table():
    poisson = 0.3
    lame = poisson / ((1.0 + poisson) * (1.0 - 2.0 * poisson))
    shear = 0.5 / (1.0 + poisson)
    elastic = np.zeros((6, 6))
    elastic[:3, :3] = lame
    for index in range(3):
        elastic[index, index] += 2.0 * shear
        elastic[index + 3, index + 3] = shear
    points = [0.5 - 0.5 / math.sqrt(3.0), 0.5 + 0.5 / math.sqrt(3.0)]
    table = np.zeros((24, 24))
    for point_z in points:
        for point_y in points:
            for point_x in points:
                strain = np.zeros((6, 24))
                for corner in range(8):
                    bit_z, bit_y, bit_x = (corner // 4, corner // 2 % 2, corner % 2)
                    shape_x = point_x if bit_x else 1.0 - point_x
                    shape_y = point_y if bit_y else 1.0 - point_y
                    shape_z = point_z if bit_z else 1.0 - point_z
                    slope_x = 1.0 if bit_x else -1.0
                    slope_y = 1.0 if bit_y else -1.0
                    slope_z = 1.0 if bit_z else -1.0
                    grad_x = slope_x * shape_y * shape_z
                    grad_y = shape_x * slope_y * shape_z
                    grad_z = shape_x * shape_y * slope_z
                    strain[0, corner] = grad_x
                    strain[1, 8 + corner] = grad_y
                    strain[2, 16 + corner] = grad_z
                    strain[3, corner] = grad_y
                    strain[3, 8 + corner] = grad_x
                    strain[4, 8 + corner] = grad_z
                    strain[4, 16 + corner] = grad_y
                    strain[5, corner] = grad_z
                    strain[5, 16 + corner] = grad_x
                table += strain.T @ elastic @ strain / 8.0
    return np.asarray(table.astype(np.float32).astype(jnp.bfloat16).astype(np.float64))


def element_matrix(table):
    matrix = np.zeros((2, 2, 2, 3, DEPTH, 2, 2, 3, DEPTH))
    for corner in range(8):
        bz, by, bx = corner // 4, corner // 2 % 2, corner % 2
        for other in range(8):
            oz, oy, ox = other // 4, other // 2 % 2, other % 2
            for c in range(3):
                for k in range(3):
                    for z in range(DEPTH - 1):
                        matrix[bz, by, bx, c, z + bz, oy, ox, k, z + oz] = table[
                            c * 8 + corner, k * 8 + other
                        ]
    return matrix.reshape(384, 192)


def depth_bands():
    bands = np.zeros((6, DEPTH, 3, DEPTH))
    for z in range(DEPTH):
        for dz in range(-2, 3):
            if 0 <= z + dz < DEPTH:
                for dy in range(3):
                    bands[KLASS.index(dz * dz + dy * dy), z, dy, z + dz] = 1.0
    return bands.reshape(96, 48)


def cone(square, dx):
    return max(0.0, 3.0 - math.sqrt(square + dx * dx))


def along_bands():
    bands = np.zeros((6, WIDE, COLS))
    for k, square in enumerate(KLASS):
        for x in range(COLS):
            for dx in range(-2, 3):
                bands[k, (x + dx) % WIDE, x] = cone(square, dx)
    return bands.reshape(6 * WIDE, COLS)


def iota(shape, dim):
    return lax.broadcasted_iota(I32, shape, dim)


def starts():
    return lax.axis_index("gy") * ROWS, lax.axis_index("gx") * COLS


def call(body, outs, ins, scratch=(), flops=0, limit=None):
    whole = pl.BlockSpec(memory_space=pltpu.VMEM)
    moved = sum(math.prod(o.shape) * o.dtype.itemsize for o in outs)
    return pl.pallas_call(
        body,
        out_shape=outs,
        in_specs=[whole] * len(ins),
        out_specs=[whole] * len(outs),
        scratch_shapes=list(scratch),
        compiler_params=pltpu.CompilerParams(vmem_limit_bytes=limit or (32 << 20)),
        cost_estimate=pl.CostEstimate(flops=flops, bytes_accessed=moved, transcendentals=0),
    )(*ins)


def shape_of(shape, dtype):
    return jax.ShapeDtypeStruct(shape, dtype)


def pack_body(grid_y, grid_x, u_ref, den_ref, sol_ref, um, st_own, co_own, low, high, uf):
    y0, x0 = starts()
    uf[...] = u_ref[...].astype(F32)
    lane = iota((DEPTH, COLS), 1)
    inside_zx = (iota((DEPTH, COLS), 0) < DEPTH - 1) & (lane + x0 < grid_x - 1)
    for y in range(ROWS):
        planes = [uf[pl.ds(c * 128 + y, DEPTH, stride=ROWS), :] for c in range(3)]
        density = den_ref[pl.ds(y, DEPTH, stride=ROWS), :]
        solid = sol_ref[pl.ds(y, DEPTH, stride=ROWS), :]
        exists = inside_zx & (y0 + y < grid_y - 1)
        physical = jnp.where(solid == 1, 1.0, density)
        square = physical * physical
        stiff = jnp.where(exists, void_modulus + (1.0 - void_modulus) * (square * physical), 0.0)
        factor = jnp.where(
            exists, (-3.0 * (1.0 - void_modulus)) * square * (1 - solid).astype(F32), 0.0
        )
        st_own[y] = stiff
        co_own[y] = factor
        planes += [stiff, factor]
        below = jnp.zeros((DEPTH, COLS), F32)
        above = jnp.zeros((DEPTH, COLS), F32)
        for p, plane in enumerate(planes):
            um[y, p] = plane.astype(BF16)
            at = SPAN * p
            moved = pltpu.roll(plane, at + LOW, 1)
            above = jnp.where((lane >= at + LOW) & (lane < at + SPAN), moved, above)
            below = jnp.where((lane >= at) & (lane < at + LOW), moved, below)
        low[y] = above.astype(BF16)
        high[y] = below.astype(BF16)


def merge_body(um, right, left, up, down, merged):
    both = (right[...].astype(F32) + left[...].astype(F32)).astype(BF16)
    merged[...] = both
    for y in range(HIGH):
        up[y * 3 : y * 3 + 3] = um[y, 0:3]
    up[15:19] = um[0:4, 3]
    up[19:21] = um[0:2, 4]
    up[21:26] = both[0:HIGH]
    for y in range(LOW):
        down[y * 3 : y * 3 + 3] = um[y + 4, 0:3]
    down[12:16] = um[4:8, 3]
    down[16:18] = um[6:8, 4]
    down[18:22] = both[4:8]


def one_hot(key, rows):
    return (iota((rows, key.shape[1]), 0) == key).astype(F32).astype(BF16)


def mask_body(grid_y, grid_x, fixed, nodes, forces, free, loads, inverse, spread):
    y0, x0 = starts()

    def keys(flat):
        x = (flat & (grid_x - 1)) - x0
        y = ((flat // grid_x) & (grid_y - 1)) - y0 + LOW
        z = flat // (grid_x * grid_y)
        near = (x >= -LOW) & (x < COLS + HIGH)
        return jnp.where(near, x & (WIDE - 1), -1), y * DEPTH + z

    def dots(a, b):
        return lax.dot_general(a, b, (((1,), (1,)), ((), ())), preferred_element_type=F32)

    count = fixed.shape[1]
    part = 512
    spread[...] = jnp.zeros_like(spread)
    for at in range(0, count, part):
        kx, ky = keys(fixed[:, at : at + part])
        spread[...] += dots(one_hot(ky, 256), one_hot(kx, WIDE))
    free[...] = jnp.where(spread[...] > 0.0, 0.0, 1.0).reshape(16, DEPTH, WIDE)

    kx, ky = keys(nodes[...])
    at_x = one_hot(kx, WIDE)
    here = iota((256, kx.shape[1]), 0) == ky
    for c in range(3):
        force = forces[c : c + 1, :]
        total = jnp.zeros((256, WIDE), F32)
        for _ in range(3):
            head = force.astype(BF16).astype(F32)
            total = total + dots(jnp.where(here, head, 0.0).astype(BF16), at_x)
            force = force - head
        loads[:, c] = total.reshape(16, DEPTH, WIDE)

    lanes = iota((DEPTH, WIDE), 1)
    xpos = x0 + jnp.where(lanes < WIDE // 2 + HIGH, lanes, lanes - WIDE)

    def within(pos, size):
        return jnp.where((pos >= 0) & (pos < size - 1), 1.0, 0.0)

    ex = [within(xpos + d, grid_x) for d in range(-2, 3)]
    rows_of = {
        k: sum(cone(k, d) * ex[d + 2] for d in range(-2, 3) if cone(k, d) > 0.0) for k in KLASS
    }
    zpos = iota((DEPTH, WIDE), 0)
    ez = [within(zpos + d, DEPTH) for d in range(-2, 3)]
    z_terms = (ez[2], ez[1] + ez[3], ez[0] + ez[4])
    for row in range(12):
        ypos = y0 + row - 2
        ey = [within(ypos + d, grid_y) for d in range(-2, 3)]
        y_terms = (ey[2], ey[1] + ey[3], ey[0] + ey[4])
        total = jnp.zeros((DEPTH, WIDE), F32)
        for a in range(3):
            inner = sum(y_terms[b] * rows_of[a * a + b * b] for b in range(3))
            total = total + z_terms[a] * inner
        alive = ez[2] * ex[2] * ey[2] > 0.0
        inverse[row] = jnp.where(alive, 1.0 / jnp.where(alive, total, 1.0), 0.0)


def main_body(
    pivot,
    um,
    st_own,
    co_own,
    merged,
    up,
    down,
    free,
    loads,
    inverse,
    matrix,
    bands_z,
    bands_x,
    smoothed,
    filtered,
    uu,
    ss,
    vv,
    st,
    st1,
    co,
    res,
    inv,
    ratio,
    layers,
    out_f,
):
    lane = iota((DEPTH, COLS), 1)
    edge = (lane < HIGH) | (lane >= COLS - LOW)

    def rim(packed, p):
        return jnp.where(edge, pltpu.roll(packed, COLS - SPAN * p - LOW, 1), 0.0)

    def put(ref, row, fields):
        ref[pl.ds(row * 96, 48), :] = fields.astype(BF16)
        ref[pl.ds(row * 96 + 48, 48), :] = pltpu.roll(fields, WIDE - 1, 1).astype(BF16)

    for row in range(17):
        n = row - LOW
        if n < 0:
            tiles = [down[row * 3 + c].astype(F32) for c in range(3)]
            packed = down[18 + row].astype(F32)
            stiff = down[12 + row].astype(F32)
            factor = down[16 + row - 2].astype(F32) if n >= -2 else None
        elif n < ROWS:
            tiles = [um[n, c].astype(F32) for c in range(3)]
            packed = merged[n].astype(F32)
            stiff, factor = st_own[n], co_own[n]
        else:
            m = n - ROWS
            tiles = [up[m * 3 + c].astype(F32) for c in range(3)]
            packed = up[21 + m].astype(F32)
            stiff = up[15 + m].astype(F32) if m < 4 else None
            factor = up[19 + m].astype(F32) if m < 2 else None
        fields = jnp.concatenate(
            [jnp.concatenate([tiles[c], rim(packed, c)], axis=1) for c in range(3)], axis=0
        )
        put(uu, row, fields)
        if stiff is not None:
            value = jnp.concatenate([stiff, rim(packed, 3)], axis=1)
            st[row] = value
            st1[row] = pltpu.roll(value, 1, 0)
        if factor is not None:
            co[row - 2] = jnp.concatenate([factor, rim(packed, 4)], axis=1)

    def forces(ref, row, carry):
        x = ref[pl.ds(row * 96, 192), :]
        f = jnp.dot(matrix[...], x, preferred_element_type=F32).reshape(2, 12, DEPTH, WIDE)
        g = (f[0] * st[row][None] + f[1] * st1[row][None]).reshape(2, 2, 3 * DEPTH, WIDE)
        h = g[0] + carry
        return h[0] + pltpu.roll(h[1], 1, 1), g[1]

    def first_step(row, carry):
        before, weight = carry
        applied, after = forces(uu, row, before)
        here = st[row] + st1[row]
        both = here + weight
        diagonal = pivot * (both + pltpu.roll(both, 1, 1))
        some = diagonal > 0.0
        inverse_diagonal = jnp.where(some, 1.0 / jnp.where(some, diagonal, 1.0), 0.0)
        inv[row] = inverse_diagonal
        mask = free[row]
        residual = (loads[row] - applied.reshape(3, DEPTH, WIDE)) * mask[None]
        res[row] = residual
        step = (residual * (inverse_diagonal * (1.0 / spectral_mid))[None]).astype(BF16)
        put(ss, row, step.astype(F32).reshape(48, WIDE))
        return after, here

    zero = jnp.zeros((2, 48, WIDE), F32)
    lax.fori_loop(0, 16, first_step, (zero, jnp.zeros((DEPTH, WIDE), F32)))

    def second_step(row, carry):
        applied, after = forces(ss, row, carry)
        step0 = ss[pl.ds(row * 96, 48), :].astype(F32).reshape(3, DEPTH, WIDE)
        old = uu[pl.ds(row * 96, 48), :].astype(F32).reshape(3, DEPTH, WIDE)
        residual = res[row] - applied.reshape(3, DEPTH, WIDE) * free[row][None]
        step1 = (second * first) * step0 + residual * (
            (2.0 * second / spectral_half) * inv[row]
        )[None]
        new = (old + step0 + step1).astype(BF16).astype(F32)
        put(vv, row, new.reshape(48, WIDE))
        return after

    lax.fori_loop(1, 15, second_step, zero)

    for y in range(ROWS):
        for c in range(3):
            out_f[pl.ds(c * 128 + y, DEPTH, stride=ROWS), :] = vv[
                (y + LOW) * 96 + c * 16 : (y + LOW) * 96 + c * 16 + 16, 0:COLS
            ].astype(F32)
    smoothed[...] = out_f[...].astype(BF16)

    def energy_step(row, carry):
        x = vv[pl.ds(row * 96, 192), :]
        f = jnp.dot(matrix[...], x, preferred_element_type=F32).reshape(2, 12, DEPTH, WIDE)
        u = x.astype(F32).reshape(12, DEPTH, WIDE)
        here = jnp.sum(f[0] * u, axis=0)
        over = jnp.sum(f[1] * u, axis=0)
        energy = here + pltpu.roll(over, DEPTH - 1, 0)
        ratio[row - 2] = energy * co[row - 2] * inverse[row - 2]
        return carry

    lax.fori_loop(2, 14, energy_step, 0)

    for y in range(ROWS):
        a = jnp.concatenate(
            [ratio[y + 2], ratio[y + 1] + ratio[y + 3], ratio[y] + ratio[y + 4]], axis=0
        )
        s = jnp.dot(bands_z[...], a.astype(BF16), preferred_element_type=F32).astype(BF16)
        for k in range(6):
            layers[y * DEPTH : (y + 1) * DEPTH, k * WIDE : (k + 1) * WIDE] = s[
                k * DEPTH : (k + 1) * DEPTH
            ]
    total = jnp.dot(layers[...], bands_x[...], preferred_element_type=F32)
    for y in range(ROWS):
        keep = jnp.where(co_own[y] < 0.0, total[y * DEPTH : (y + 1) * DEPTH], 0.0)
        filtered[pl.ds(y, DEPTH, stride=ROWS), :] = keep


def passed_along(shard, axis, by):
    size = lax.axis_size(axis)
    return lax.ppermute(shard, axis, [(i, i + by) for i in range(size) if 0 <= i + by < size])


def shards(displacement, density, solid, fixed_nodes, load_nodes, load_forces):
    grid_y = ROWS * lax.axis_size("gy")
    grid_x = COLS * lax.axis_size("gx")
    table = stiffness_table()
    pivot = float(table[0, 0])
    tile = (DEPTH, COLS)

    um, st_own, co_own, low, high = call(
        lambda *refs: pack_body(grid_y, grid_x, *refs),
        [
            shape_of((ROWS, 5) + tile, BF16),
            shape_of((ROWS,) + tile, F32),
            shape_of((ROWS,) + tile, F32),
            shape_of((ROWS,) + tile, BF16),
            shape_of((ROWS,) + tile, BF16),
        ],
        [displacement.reshape(384, 128), density.reshape(128, 128), solid.reshape(128, 128)],
        [pltpu.VMEM((384, 128), F32)],
    )
    right = passed_along(low, "gx", -1)
    left = passed_along(high, "gx", 1)
    free, loads, inverse = call(
        lambda *refs: mask_body(grid_y, grid_x, *refs),
        [
            shape_of((16, DEPTH, WIDE), F32),
            shape_of((16, 3, DEPTH, WIDE), F32),
            shape_of((12, DEPTH, WIDE), F32),
        ],
        [fixed_nodes.reshape(1, -1), load_nodes.reshape(1, -1), load_forces.T],
        [pltpu.VMEM((256, WIDE), F32)],
        flops=2000000000,
    )
    up, down, merged = call(
        merge_body,
        [
            shape_of((26,) + tile, BF16),
            shape_of((22,) + tile, BF16),
            shape_of((ROWS,) + tile, BF16),
        ],
        [um, right, left],
    )
    from_above = passed_along(up, "gy", -1)
    from_below = passed_along(down, "gy", 1)
    smoothed, filtered = call(
        lambda *refs: main_body(pivot, *refs),
        [shape_of((384, 128), BF16), shape_of((128, 128), F32)],
        [
            um,
            st_own,
            co_own,
            merged,
            from_above,
            from_below,
            free,
            loads,
            inverse,
            jnp.asarray(element_matrix(table), BF16),
            jnp.asarray(depth_bands(), BF16),
            jnp.asarray(along_bands(), BF16),
        ],
        [
            pltpu.VMEM((17 * 96, WIDE), BF16),
            pltpu.VMEM((16 * 96, WIDE), BF16),
            pltpu.VMEM((15 * 96, WIDE), BF16),
            pltpu.VMEM((16, DEPTH, WIDE), F32),
            pltpu.VMEM((16, DEPTH, WIDE), F32),
            pltpu.VMEM((12, DEPTH, WIDE), F32),
            pltpu.VMEM((16, 3, DEPTH, WIDE), F32),
            pltpu.VMEM((16, DEPTH, WIDE), F32),
            pltpu.VMEM((12, DEPTH, WIDE), F32),
            pltpu.VMEM((128, 6 * WIDE), BF16),
            pltpu.VMEM((384, 128), F32),
        ],
        flops=10000000000,
    )
    return smoothed.reshape(3, DEPTH, ROWS, COLS), filtered.reshape(DEPTH, ROWS, COLS)


def solution(mesh):
    placed = (P(None, None, "gy", "gx"), P(None, "gy", "gx"), P(None, "gy", "gx"), P(), P(), P())
    return jax.shard_map(
        shards,
        mesh=mesh,
        in_specs=placed,
        out_specs=(P(None, None, "gy", "gx"), P(None, "gy", "gx")),
        check_vma=False,
    )
```

```python
import math

import jax
import jax.numpy as jnp
import numpy as np
from jax import lax
from jax.experimental import pallas as pl
from jax.experimental.pallas import tpu as pltpu
from jax.sharding import PartitionSpec as P

void_modulus = 0.001
spectral_mid = 1.375
spectral_half = 1.125
sigma = spectral_mid / spectral_half
first = 1.0 / sigma
second = 1.0 / (2.0 * sigma - first)

F32, BF16, I32 = jnp.float32, jnp.bfloat16, jnp.int32
DEPTH, ROWS, COLS = 16, 8, 128
LOW, HIGH = 4, 5
WIDE = 256
SPAN = LOW + HIGH
KLASS = (0, 1, 2, 4, 5, 8)


def stiffness_table():
    poisson = 0.3
    lame = poisson / ((1.0 + poisson) * (1.0 - 2.0 * poisson))
    shear = 0.5 / (1.0 + poisson)
    elastic = np.zeros((6, 6))
    elastic[:3, :3] = lame
    for index in range(3):
        elastic[index, index] += 2.0 * shear
        elastic[index + 3, index + 3] = shear
    points = [0.5 - 0.5 / math.sqrt(3.0), 0.5 + 0.5 / math.sqrt(3.0)]
    table = np.zeros((24, 24))
    for point_z in points:
        for point_y in points:
            for point_x in points:
                strain = np.zeros((6, 24))
                for corner in range(8):
                    bit_z, bit_y, bit_x = (corner // 4, corner // 2 % 2, corner % 2)
                    shape_x = point_x if bit_x else 1.0 - point_x
                    shape_y = point_y if bit_y else 1.0 - point_y
                    shape_z = point_z if bit_z else 1.0 - point_z
                    slope_x = 1.0 if bit_x else -1.0
                    slope_y = 1.0 if bit_y else -1.0
                    slope_z = 1.0 if bit_z else -1.0
                    grad_x = slope_x * shape_y * shape_z
                    grad_y = shape_x * slope_y * shape_z
                    grad_z = shape_x * shape_y * slope_z
                    strain[0, corner] = grad_x
                    strain[1, 8 + corner] = grad_y
                    strain[2, 16 + corner] = grad_z
                    strain[3, corner] = grad_y
                    strain[3, 8 + corner] = grad_x
                    strain[4, 8 + corner] = grad_z
                    strain[4, 16 + corner] = grad_y
                    strain[5, corner] = grad_z
                    strain[5, 16 + corner] = grad_x
                table += strain.T @ elastic @ strain / 8.0
    return np.asarray(table.astype(np.float32).astype(jnp.bfloat16).astype(np.float64))


def element_matrix(table):
    matrix = np.zeros((2, 2, 2, 3, DEPTH, 2, 2, 3, DEPTH))
    for corner in range(8):
        bz, by, bx = corner // 4, corner // 2 % 2, corner % 2
        for other in range(8):
            oz, oy, ox = other // 4, other // 2 % 2, other % 2
            for c in range(3):
                for k in range(3):
                    for z in range(DEPTH - 1):
                        matrix[bz, by, bx, c, z + bz, oy, ox, k, z + oz] = table[
                            c * 8 + corner, k * 8 + other
                        ]
    return matrix.reshape(384, 192)


def depth_bands():
    bands = np.zeros((6, DEPTH, 3, DEPTH))
    for z in range(DEPTH):
        for dz in range(-2, 3):
            if 0 <= z + dz < DEPTH:
                for dy in range(3):
                    bands[KLASS.index(dz * dz + dy * dy), z, dy, z + dz] = 1.0
    return bands.reshape(96, 48)


def cone(square, dx):
    return max(0.0, 3.0 - math.sqrt(square + dx * dx))


def along_bands():
    bands = np.zeros((6, WIDE, COLS))
    for k, square in enumerate(KLASS):
        for x in range(COLS):
            for dx in range(-2, 3):
                bands[k, (x + dx) % WIDE, x] = cone(square, dx)
    return bands.reshape(6 * WIDE, COLS)


def iota(shape, dim):
    return lax.broadcasted_iota(I32, shape, dim)


def starts():
    return lax.axis_index("gy") * ROWS, lax.axis_index("gx") * COLS


def call(body, outs, ins, scratch=(), flops=0, limit=None, space=pltpu.VMEM):
    whole = pl.BlockSpec(memory_space=pltpu.VMEM)
    moved = sum(math.prod(o.shape) * o.dtype.itemsize for o in outs)
    return pl.pallas_call(
        body,
        out_shape=outs,
        in_specs=[pl.BlockSpec(memory_space=space)] * len(ins),
        out_specs=[whole] * len(outs),
        scratch_shapes=list(scratch),
        compiler_params=pltpu.CompilerParams(vmem_limit_bytes=limit or (32 << 20)),
        cost_estimate=pl.CostEstimate(flops=flops, bytes_accessed=moved, transcendentals=0),
    )(*ins)


def shape_of(shape, dtype):
    return jax.ShapeDtypeStruct(shape, dtype)


def pack_body(
    grid_y, grid_x, u_in, den_in, sol_in, um, st_own, co_own, far, near, u_ref, den_ref, sol_ref, uf, sem
):
    copies = [
        pltpu.make_async_copy(source, target, sem.at[i])
        for i, (source, target) in enumerate(
            ((u_in, u_ref), (den_in, den_ref), (sol_in, sol_ref))
        )
    ]
    for copy in copies:
        copy.start()
    y0, x0 = starts()
    odd = lax.axis_index("gx") % 2 == 1
    for copy in copies:
        copy.wait()
    uf[...] = u_ref[...].astype(F32)
    lane = iota((DEPTH, COLS), 1)
    inside_zx = (iota((DEPTH, COLS), 0) < DEPTH - 1) & (lane + x0 < grid_x - 1)
    for y in range(ROWS):
        planes = [uf[pl.ds(c * 128 + y, DEPTH, stride=ROWS), :] for c in range(3)]
        density = den_ref[pl.ds(y, DEPTH, stride=ROWS), :]
        solid = sol_ref[pl.ds(y, DEPTH, stride=ROWS), :]
        exists = inside_zx & (y0 + y < grid_y - 1)
        physical = jnp.where(solid == 1, 1.0, density)
        square = physical * physical
        stiff = jnp.where(exists, void_modulus + (1.0 - void_modulus) * (square * physical), 0.0)
        factor = jnp.where(
            exists, (-3.0 * (1.0 - void_modulus)) * square * (1 - solid).astype(F32), 0.0
        )
        st_own[y] = stiff
        co_own[y] = factor
        planes += [stiff, factor]
        below = jnp.zeros((DEPTH, COLS), F32)
        above = jnp.zeros((DEPTH, COLS), F32)
        for p, plane in enumerate(planes):
            um[y, p] = plane.astype(BF16)
            at = SPAN * p
            moved = pltpu.roll(plane, at + LOW, 1)
            above = jnp.where((lane >= at + LOW) & (lane < at + SPAN), moved, above)
            below = jnp.where((lane >= at) & (lane < at + LOW), moved, below)
        far[y] = jnp.where(odd, below, above).astype(BF16)
        near[y] = jnp.where(odd, above, below).astype(BF16)


def merge_body(um, from_far, from_near, far, near, merged):
    both = (from_far[...].astype(F32) + from_near[...].astype(F32)).astype(BF16)
    merged[...] = both

    def fill(up, down):
        for y in range(HIGH):
            up[y * 3 : y * 3 + 3] = um[y, 0:3]
        up[15:19] = um[0:4, 3]
        up[19:21] = um[0:2, 4]
        up[21:26] = both[0:HIGH]
        for y in range(LOW):
            down[y * 3 : y * 3 + 3] = um[y + 4, 0:3]
        down[12:16] = um[4:8, 3]
        down[16:18] = um[6:8, 4]
        down[18:22] = both[4:8]
        down[22:26] = jnp.zeros((4, DEPTH, COLS), BF16)

    odd = lax.axis_index("gy") % 2 == 1
    pl.when(odd)(lambda: fill(near, far))
    pl.when(jnp.logical_not(odd))(lambda: fill(far, near))


def one_hot(key, rows):
    return (iota((rows, key.shape[1]), 0) == key).astype(F32).astype(BF16)


def mask_body(grid_y, grid_x, fixed, nodes, forces, free, loads, inverse, spread):
    y0, x0 = starts()

    def keys(flat):
        x = (flat & (grid_x - 1)) - x0
        y = ((flat // grid_x) & (grid_y - 1)) - y0 + LOW
        z = flat // (grid_x * grid_y)
        near = (x >= -LOW) & (x < COLS + HIGH)
        return jnp.where(near, x & (WIDE - 1), -1), y * DEPTH + z

    def dots(a, b):
        return lax.dot_general(a, b, (((1,), (1,)), ((), ())), preferred_element_type=F32)

    count = fixed.shape[1]
    part = 512
    spread[...] = jnp.zeros_like(spread)
    for at in range(0, count, part):
        kx, ky = keys(fixed[:, at : at + part])
        spread[...] += dots(one_hot(ky, 256), one_hot(kx, WIDE))
    free[...] = jnp.where(spread[...] > 0.0, 0.0, 1.0).reshape(16, DEPTH, WIDE)

    kx, ky = keys(nodes[...])
    at_x = one_hot(kx, WIDE)
    here = iota((256, kx.shape[1]), 0) == ky
    for c in range(3):
        force = forces[c : c + 1, :]
        total = jnp.zeros((256, WIDE), F32)
        for _ in range(3):
            head = force.astype(BF16).astype(F32)
            total = total + dots(jnp.where(here, head, 0.0).astype(BF16), at_x)
            force = force - head
        loads[:, c] = total.reshape(16, DEPTH, WIDE)

    lanes = iota((DEPTH, WIDE), 1)
    xpos = x0 + jnp.where(lanes < WIDE // 2 + HIGH, lanes, lanes - WIDE)

    def within(pos, size):
        return jnp.where((pos >= 0) & (pos < size - 1), 1.0, 0.0)

    ex = [within(xpos + d, grid_x) for d in range(-2, 3)]
    rows_of = {
        k: sum(cone(k, d) * ex[d + 2] for d in range(-2, 3) if cone(k, d) > 0.0) for k in KLASS
    }
    zpos = iota((DEPTH, WIDE), 0)
    ez = [within(zpos + d, DEPTH) for d in range(-2, 3)]
    z_terms = (ez[2], ez[1] + ez[3], ez[0] + ez[4])
    for row in range(12):
        ypos = y0 + row - 2
        ey = [within(ypos + d, grid_y) for d in range(-2, 3)]
        y_terms = (ey[2], ey[1] + ey[3], ey[0] + ey[4])
        total = jnp.zeros((DEPTH, WIDE), F32)
        for a in range(3):
            inner = sum(y_terms[b] * rows_of[a * a + b * b] for b in range(3))
            total = total + z_terms[a] * inner
        alive = ez[2] * ex[2] * ey[2] > 0.0
        inverse[row] = jnp.where(alive, 1.0 / jnp.where(alive, total, 1.0), 0.0)


def main_body(
    pivot,
    um,
    st_own,
    co_own,
    merged,
    from_far,
    from_near,
    free,
    loads,
    inverse,
    matrix,
    bands_z,
    bands_x,
    smoothed,
    filtered,
    uu,
    ss,
    vv,
    st,
    st1,
    co,
    res,
    inv,
    ratio,
    layers,
    out_f,
):
    odd = lax.axis_index("gy") % 2 == 1
    lane = iota((DEPTH, COLS), 1)

    def above(i):
        return jnp.where(odd, from_far[i].astype(F32), from_near[i].astype(F32))

    def below(i):
        return jnp.where(odd, from_near[i].astype(F32), from_far[i].astype(F32))

    edge = (lane < HIGH) | (lane >= COLS - LOW)

    def rim(packed, p):
        return jnp.where(edge, pltpu.roll(packed, COLS - SPAN * p - LOW, 1), 0.0)

    def put(ref, row, fields):
        ref[pl.ds(row * 96, 48), :] = fields.astype(BF16)
        ref[pl.ds(row * 96 + 48, 48), :] = pltpu.roll(fields, WIDE - 1, 1).astype(BF16)

    for row in range(17):
        n = row - LOW
        if n < 0:
            tiles = [below(row * 3 + c) for c in range(3)]
            packed = below(18 + row)
            stiff = below(12 + row)
            factor = below(16 + row - 2) if n >= -2 else None
        elif n < ROWS:
            tiles = [um[n, c].astype(F32) for c in range(3)]
            packed = merged[n].astype(F32)
            stiff, factor = st_own[n], co_own[n]
        else:
            m = n - ROWS
            tiles = [above(m * 3 + c) for c in range(3)]
            packed = above(21 + m)
            stiff = above(15 + m) if m < 4 else None
            factor = above(19 + m) if m < 2 else None
        fields = jnp.concatenate(
            [jnp.concatenate([tiles[c], rim(packed, c)], axis=1) for c in range(3)], axis=0
        )
        put(uu, row, fields)
        if stiff is not None:
            value = jnp.concatenate([stiff, rim(packed, 3)], axis=1)
            st[row] = value
            st1[row] = pltpu.roll(value, 1, 0)
        if factor is not None:
            co[row - 2] = jnp.concatenate([factor, rim(packed, 4)], axis=1)

    def forces(ref, row, carry):
        x = ref[pl.ds(row * 96, 192), :]
        f = jnp.dot(matrix[...], x, preferred_element_type=F32).reshape(2, 12, DEPTH, WIDE)
        g = (f[0] * st[row][None] + f[1] * st1[row][None]).reshape(2, 2, 3 * DEPTH, WIDE)
        h = g[0] + carry
        return h[0] + pltpu.roll(h[1], 1, 1), g[1]

    def first_step(row, carry):
        before, weight = carry
        applied, after = forces(uu, row, before)
        here = st[row] + st1[row]
        both = here + weight
        diagonal = pivot * (both + pltpu.roll(both, 1, 1))
        some = diagonal > 0.0
        inverse_diagonal = jnp.where(some, 1.0 / jnp.where(some, diagonal, 1.0), 0.0)
        inv[row] = inverse_diagonal
        mask = free[row]
        residual = (loads[row] - applied.reshape(3, DEPTH, WIDE)) * mask[None]
        res[row] = residual
        step = (residual * (inverse_diagonal * (1.0 / spectral_mid))[None]).astype(BF16)
        put(ss, row, step.astype(F32).reshape(48, WIDE))
        return after, here

    zero = jnp.zeros((2, 48, WIDE), F32)
    lax.fori_loop(0, 16, first_step, (zero, jnp.zeros((DEPTH, WIDE), F32)), unroll=4)

    def second_step(row, carry):
        applied, after = forces(ss, row, carry)
        step0 = ss[pl.ds(row * 96, 48), :].astype(F32).reshape(3, DEPTH, WIDE)
        old = uu[pl.ds(row * 96, 48), :].astype(F32).reshape(3, DEPTH, WIDE)
        residual = res[row] - applied.reshape(3, DEPTH, WIDE) * free[row][None]
        step1 = (second * first) * step0 + residual * (
            (2.0 * second / spectral_half) * inv[row]
        )[None]
        new = (old + step0 + step1).astype(BF16).astype(F32)
        put(vv, row, new.reshape(48, WIDE))
        return after

    lax.fori_loop(1, 15, second_step, zero, unroll=4)

    for y in range(ROWS):
        for c in range(3):
            out_f[pl.ds(c * 128 + y, DEPTH, stride=ROWS), :] = vv[
                (y + LOW) * 96 + c * 16 : (y + LOW) * 96 + c * 16 + 16, 0:COLS
            ].astype(F32)
    smoothed[...] = out_f[...].astype(BF16)

    def energy_step(row, carry):
        x = vv[pl.ds(row * 96, 192), :]
        f = jnp.dot(matrix[...], x, preferred_element_type=F32).reshape(2, 12, DEPTH, WIDE)
        u = x.astype(F32).reshape(12, DEPTH, WIDE)
        here = jnp.sum(f[0] * u, axis=0)
        over = jnp.sum(f[1] * u, axis=0)
        energy = here + pltpu.roll(over, DEPTH - 1, 0)
        ratio[row - 2] = energy * co[row - 2] * inverse[row - 2]
        return carry

    lax.fori_loop(2, 14, energy_step, 0, unroll=4)

    for y in range(ROWS):
        a = jnp.concatenate(
            [ratio[y + 2], ratio[y + 1] + ratio[y + 3], ratio[y] + ratio[y + 4]], axis=0
        )
        s = jnp.dot(bands_z[...], a.astype(BF16), preferred_element_type=F32).astype(BF16)
        for k in range(6):
            layers[y * DEPTH : (y + 1) * DEPTH, k * WIDE : (k + 1) * WIDE] = s[
                k * DEPTH : (k + 1) * DEPTH
            ]
    total = jnp.dot(layers[...], bands_x[...], preferred_element_type=F32)
    for y in range(ROWS):
        keep = jnp.where(co_own[y] < 0.0, total[y * DEPTH : (y + 1) * DEPTH], 0.0)
        filtered[pl.ds(y, DEPTH, stride=ROWS), :] = keep


def swapped(shard, axis, odd):
    size = lax.axis_size(axis)
    partner = [((i - odd) ^ 1) + odd for i in range(size)]
    return lax.ppermute(shard, axis, [(i, j) for i, j in enumerate(partner) if 0 <= j < size])


def shards(displacement, density, solid, fixed_nodes, load_nodes, load_forces):
    grid_y = ROWS * lax.axis_size("gy")
    grid_x = COLS * lax.axis_size("gx")
    table = stiffness_table()
    pivot = float(table[0, 0])
    tile = (DEPTH, COLS)

    um, st_own, co_own, far, near = call(
        lambda *refs: pack_body(grid_y, grid_x, *refs),
        [
            shape_of((ROWS, 5) + tile, BF16),
            shape_of((ROWS,) + tile, F32),
            shape_of((ROWS,) + tile, F32),
            shape_of((ROWS,) + tile, BF16),
            shape_of((ROWS,) + tile, BF16),
        ],
        [
            pltpu.with_memory_space_constraint(a, pltpu.HBM)
            for a in (displacement.reshape(384, 128), density.reshape(128, 128), solid.reshape(128, 128))
        ],
        [
            pltpu.VMEM((384, 128), BF16),
            pltpu.VMEM((128, 128), F32),
            pltpu.VMEM((128, 128), I32),
            pltpu.VMEM((384, 128), F32),
            pltpu.SemaphoreType.DMA((3,)),
        ],
        space=pltpu.HBM,
    )
    nodes, _ = lax.optimization_barrier((fixed_nodes, far))
    from_far = swapped(far, "gx", 1)
    from_near = swapped(near, "gx", 0)
    free, loads, inverse = call(
        lambda *refs: mask_body(grid_y, grid_x, *refs),
        [
            shape_of((16, DEPTH, WIDE), F32),
            shape_of((16, 3, DEPTH, WIDE), F32),
            shape_of((12, DEPTH, WIDE), F32),
        ],
        [nodes.reshape(1, -1), load_nodes.reshape(1, -1), load_forces.T],
        [pltpu.VMEM((256, WIDE), F32)],
        flops=2000000000,
    )
    from_far, from_near, free = lax.optimization_barrier((from_far, from_near, free))
    far, near, merged = call(
        merge_body,
        [
            shape_of((26,) + tile, BF16),
            shape_of((26,) + tile, BF16),
            shape_of((ROWS,) + tile, BF16),
        ],
        [um, from_far, from_near],
    )
    from_far = swapped(far, "gy", 1)
    from_near = swapped(near, "gy", 0)
    smoothed, filtered = call(
        lambda *refs: main_body(pivot, *refs),
        [shape_of((384, 128), BF16), shape_of((128, 128), F32)],
        [
            um,
            st_own,
            co_own,
            merged,
            from_far,
            from_near,
            free,
            loads,
            inverse,
            jnp.asarray(element_matrix(table), BF16),
            jnp.asarray(depth_bands(), BF16),
            jnp.asarray(along_bands(), BF16),
        ],
        [
            pltpu.VMEM((17 * 96, WIDE), BF16),
            pltpu.VMEM((16 * 96, WIDE), BF16),
            pltpu.VMEM((15 * 96, WIDE), BF16),
            pltpu.VMEM((16, DEPTH, WIDE), F32),
            pltpu.VMEM((16, DEPTH, WIDE), F32),
            pltpu.VMEM((12, DEPTH, WIDE), F32),
            pltpu.VMEM((16, 3, DEPTH, WIDE), F32),
            pltpu.VMEM((16, DEPTH, WIDE), F32),
            pltpu.VMEM((12, DEPTH, WIDE), F32),
            pltpu.VMEM((128, 6 * WIDE), BF16),
            pltpu.VMEM((384, 128), F32),
        ],
        flops=10000000000,
    )
    return smoothed.reshape(3, DEPTH, ROWS, COLS), filtered.reshape(DEPTH, ROWS, COLS)


def solution(mesh):
    placed = (P(None, None, "gy", "gx"), P(None, "gy", "gx"), P(None, "gy", "gx"), P(), P(), P())
    return jax.shard_map(
        shards,
        mesh=mesh,
        in_specs=placed,
        out_specs=(P(None, None, "gy", "gx"), P(None, "gy", "gx")),
        check_vma=False,
    )
```

```python
import math

import jax
import jax.numpy as jnp
import numpy as np
from jax import lax
from jax.experimental import pallas as pl
from jax.experimental.pallas import tpu as pltpu
from jax.sharding import PartitionSpec as P

void_modulus = 0.001
spectral_mid = 1.375
spectral_half = 1.125
sigma = spectral_mid / spectral_half
first = 1.0 / sigma
second = 1.0 / (2.0 * sigma - first)

F32, BF16, I32 = jnp.float32, jnp.bfloat16, jnp.int32
DEPTH, ROWS, COLS = 16, 8, 128
LOW, HIGH = 4, 5
WIDE, SLOT, SEAM = 256, 117, 120
OWN = COLS - SLOT
UNROLL = (8, 7, 6)
KLASS = (0, 1, 2, 4, 5, 8)


def stiffness_table():
    poisson = 0.3
    lame = poisson / ((1.0 + poisson) * (1.0 - 2.0 * poisson))
    shear = 0.5 / (1.0 + poisson)
    elastic = np.zeros((6, 6))
    elastic[:3, :3] = lame
    for index in range(3):
        elastic[index, index] += 2.0 * shear
        elastic[index + 3, index + 3] = shear
    points = [0.5 - 0.5 / math.sqrt(3.0), 0.5 + 0.5 / math.sqrt(3.0)]
    table = np.zeros((24, 24))
    for point_z in points:
        for point_y in points:
            for point_x in points:
                strain = np.zeros((6, 24))
                for corner in range(8):
                    bit_z, bit_y, bit_x = (corner // 4, corner // 2 % 2, corner % 2)
                    shape_x = point_x if bit_x else 1.0 - point_x
                    shape_y = point_y if bit_y else 1.0 - point_y
                    shape_z = point_z if bit_z else 1.0 - point_z
                    slope_x = 1.0 if bit_x else -1.0
                    slope_y = 1.0 if bit_y else -1.0
                    slope_z = 1.0 if bit_z else -1.0
                    grad_x = slope_x * shape_y * shape_z
                    grad_y = shape_x * slope_y * shape_z
                    grad_z = shape_x * shape_y * slope_z
                    strain[0, corner] = grad_x
                    strain[1, 8 + corner] = grad_y
                    strain[2, 16 + corner] = grad_z
                    strain[3, corner] = grad_y
                    strain[3, 8 + corner] = grad_x
                    strain[4, 8 + corner] = grad_z
                    strain[4, 16 + corner] = grad_y
                    strain[5, corner] = grad_z
                    strain[5, 16 + corner] = grad_x
                table += strain.T @ elastic @ strain / 8.0
    return np.asarray(table.astype(np.float32).astype(jnp.bfloat16).astype(np.float64))


def element_matrix(table):
    matrix = np.zeros((2, 2, 2, 3, DEPTH, 2, 2, 3, DEPTH))
    for corner in range(8):
        bz, by, bx = corner // 4, corner // 2 % 2, corner % 2
        for other in range(8):
            oz, oy, ox = other // 4, other // 2 % 2, other % 2
            for c in range(3):
                for k in range(3):
                    for z in range(DEPTH - 1):
                        matrix[bz, by, bx, c, z + bz, oy, ox, k, z + oz] = table[
                            c * 8 + corner, k * 8 + other
                        ]
    return matrix.reshape(384, 192)


def depth_bands():
    bands = np.zeros((6, DEPTH, 3, DEPTH))
    for z in range(DEPTH):
        for dz in range(-2, 3):
            if 0 <= z + dz < DEPTH:
                for dy in range(3):
                    bands[KLASS.index(dz * dz + dy * dy), z, dy, z + dz] = 1.0
    return bands.reshape(96, 48)


def cone(square, dx):
    return max(0.0, 3.0 - math.sqrt(square + dx * dx))


def along_bands():
    bands = np.zeros((6, WIDE, COLS))
    for k, square in enumerate(KLASS):
        for x in range(COLS):
            for dx in range(-2, 3):
                at = x + dx
                lane = at + LOW if at <= SEAM else COLS + at - SLOT
                bands[k, lane, x] = cone(square, dx)
    return bands.reshape(6 * WIDE, COLS)


def iota(shape, dim):
    return lax.broadcasted_iota(I32, shape, dim)


def starts():
    return lax.axis_index("gy") * ROWS, lax.axis_index("gx") * COLS


def call(body, outs, ins, scratch=(), flops=0, limit=None, space=pltpu.VMEM):
    whole = pl.BlockSpec(memory_space=pltpu.VMEM)
    moved = sum(math.prod(o.shape) * o.dtype.itemsize for o in outs)
    return pl.pallas_call(
        body,
        out_shape=outs,
        in_specs=[pl.BlockSpec(memory_space=space)] * len(ins),
        out_specs=[whole] * len(outs),
        scratch_shapes=list(scratch),
        compiler_params=pltpu.CompilerParams(vmem_limit_bytes=limit or (32 << 20)),
        cost_estimate=pl.CostEstimate(flops=flops, bytes_accessed=moved, transcendentals=0),
    )(*ins)


def shape_of(shape, dtype):
    return jax.ShapeDtypeStruct(shape, dtype)


def slot_of(y):
    return 16 * ((y + LOW) % 8)


def pack_body(
    grid_y, grid_x, u_in, den_in, sol_in,
    um, st_own, co_own, keep, own, far, near, u_ref, den_ref, sol_ref, uf, sem,
):
    copies = [
        pltpu.make_async_copy(source, target, sem.at[i])
        for i, (source, target) in enumerate(
            ((u_in, u_ref), (den_in, den_ref), (sol_in, sol_ref))
        )
    ]
    for copy in copies:
        copy.start()
    y0, x0 = starts()
    odd = lax.axis_index("gx") % 2 == 1
    for copy in copies:
        copy.wait()
    uf[...] = u_ref[...].astype(F32)
    lane = iota((DEPTH, COLS), 1)
    inside_zx = (iota((DEPTH, COLS), 0) < DEPTH - 1) & (lane + x0 < grid_x - 1)
    blank = jnp.zeros((DEPTH, COLS), F32)
    middle, above, below = [blank] * 5, [blank] * 5, [blank] * 5
    for y in range(ROWS):
        planes = [uf[pl.ds(c * 128 + y, DEPTH, stride=ROWS), :] for c in range(3)]
        density = den_ref[pl.ds(y, DEPTH, stride=ROWS), :]
        solid = sol_ref[pl.ds(y, DEPTH, stride=ROWS), :]
        exists = inside_zx & (y0 + y < grid_y - 1)
        physical = jnp.where(solid == 1, 1.0, density)
        square = physical * physical
        stiff = jnp.where(exists, void_modulus + (1.0 - void_modulus) * (square * physical), 0.0)
        designed = (1 - solid).astype(F32)
        factor = jnp.where(exists, (-3.0 * (1.0 - void_modulus)) * square * designed, 0.0)
        keep[y] = jnp.where(exists, designed, 0.0)
        planes += [stiff, factor]
        at = slot_of(y)
        for p, plane in enumerate(planes):
            tile = pltpu.roll(plane, LOW, 1)
            um[y, p] = tile.astype(BF16)
            if p == 3:
                st_own[y] = tile
            if p == 4:
                co_own[y] = tile
            moved = pltpu.roll(plane, at + OWN, 1)
            middle[p] = jnp.where((lane >= at) & (lane < at + OWN), moved, middle[p])
            above[p] = jnp.where((lane >= at + OWN) & (lane < at + 16), moved, above[p])
            moved = pltpu.roll(plane, (at + LOW) % COLS, 1)
            below[p] = jnp.where((lane >= at) & (lane < at + LOW), moved, below[p])
    for p in range(5):
        own[p] = middle[p].astype(BF16)
        far[p] = jnp.where(odd, below[p], above[p]).astype(BF16)
        near[p] = jnp.where(odd, above[p], below[p]).astype(BF16)


def merge_body(um, st_own, co_own, own, from_far, from_near, far, near, tiles, st, co, slots):
    odd_x = lax.axis_index("gx") % 2 == 1
    edge = iota((DEPTH, COLS), 1) < LOW
    for p in range(5):
        one, other = from_far[p].astype(F32), from_near[p].astype(F32)
        right, left = jnp.where(odd_x, one, other), jnp.where(odd_x, other, one)
        slots[p] = (own[p].astype(F32) + right).astype(BF16)
        for y in range(ROWS):
            rim = pltpu.roll(left, (COLS - slot_of(y)) % COLS, 1)
            tiles[y, p] = jnp.where(edge, rim, um[y, p].astype(F32)).astype(BF16)
            if p == 3:
                st[y] = jnp.where(edge, rim, st_own[y])
            if p == 4:
                co[y] = jnp.where(edge, rim, co_own[y])

    def fill(up, down):
        for y in range(HIGH):
            up[y * 3 : y * 3 + 3] = tiles[y, 0:3]
        up[15:19] = tiles[0:4, 3]
        up[19:21] = tiles[0:2, 4]
        up[21:26] = slots[...]
        for y in range(LOW):
            down[y * 3 : y * 3 + 3] = tiles[y + 4, 0:3]
        down[12:16] = tiles[4:8, 3]
        down[16:18] = tiles[6:8, 4]
        down[18:21] = jnp.zeros((3, DEPTH, COLS), BF16)
        down[21:26] = slots[...]

    odd = lax.axis_index("gy") % 2 == 1
    pl.when(odd)(lambda: fill(near, far))
    pl.when(jnp.logical_not(odd))(lambda: fill(far, near))


def one_hot(key, rows):
    return (iota((rows, key.shape[1]), 0) == key).astype(F32).astype(BF16)


def mask_body(
    grid_y, grid_x, fixed, nodes, forces, free, free_b, loads, loads_b, inverse, inverse_b, spread
):
    y0, x0 = starts()
    lane = iota((DEPTH, COLS), 1)

    def keys(flat):
        x = (flat & (grid_x - 1)) - x0
        y = ((flat // grid_x) & (grid_y - 1)) - y0 + LOW
        z = flat // (grid_x * grid_y)
        slot = jnp.where((x >= SLOT) & (x < SLOT + 16), x - SLOT, -1)
        places = jnp.concatenate([one_hot(x + LOW, COLS), one_hot(slot, COLS)], axis=0)
        return places, y * DEPTH + z

    def dots(a, b):
        return lax.dot_general(a, b, (((1,), (1,)), ((), ())), preferred_element_type=F32)

    def split(total):
        rows = total.reshape(16, DEPTH, WIDE)
        halves = [jnp.zeros((DEPTH, COLS), F32)] * 2
        for row in range(16):
            at = 16 * (row % 8)
            moved = pltpu.roll(rows[row, :, COLS:], at, 1)
            halves[row // 8] = jnp.where((lane >= at) & (lane < at + 16), moved, halves[row // 8])
        return rows[:, :, :COLS], jnp.concatenate(halves, axis=1)

    count = fixed.shape[1]
    part = 512
    spread[...] = jnp.zeros_like(spread)
    for at in range(0, count, part):
        kx, ky = keys(fixed[:, at : at + part])
        spread[...] += dots(one_hot(ky, 256), kx)
    free[...], free_b[...] = split(jnp.where(spread[...] > 0.0, 0.0, 1.0))

    at_x, ky = keys(nodes[...])
    here = iota((256, ky.shape[1]), 0) == ky
    for c in range(3):
        force = forces[c : c + 1, :]
        total = jnp.zeros((256, WIDE), F32)
        for _ in range(3):
            head = force.astype(BF16).astype(F32)
            total = total + dots(jnp.where(here, head, 0.0).astype(BF16), at_x)
            force = force - head
        loads[:, c], loads_b[c] = split(total)

    def within(pos, size):
        return jnp.where((pos >= 0) & (pos < size - 1), 1.0, 0.0)

    def along(xpos):
        ex = [within(xpos + d, grid_x) for d in range(-2, 3)]
        reach = {
            k: sum(cone(k, d) * ex[d + 2] for d in range(-2, 3) if cone(k, d) > 0.0)
            for k in KLASS
        }
        return ex[2], reach

    def around(pos, size):
        e = [within(pos + d, size) for d in range(-2, 3)]
        return e[2], e[1] + e[3], e[0] + e[4]

    def reciprocal(z_terms, y_terms, x_here, reach):
        total = 0.0
        for a in range(3):
            total = total + z_terms[a] * sum(y_terms[b] * reach[a * a + b * b] for b in range(3))
        alive = z_terms[0] * x_here * y_terms[0] > 0.0
        return jnp.where(alive, 1.0 / jnp.where(alive, total, 1.0), 0.0)

    x_here, reach = along(x0 + lane - LOW)
    z_terms = around(iota((DEPTH, COLS), 0), DEPTH)
    for row in range(12):
        inverse[row] = reciprocal(z_terms, around(y0 + row - 2, grid_y), x_here, reach)
    wide = iota((DEPTH, WIDE), 1)
    x_here, reach = along(x0 + SLOT + (wide & 15))
    z_terms = around(iota((DEPTH, WIDE), 0), DEPTH)
    inverse_b[...] = reciprocal(z_terms, around(y0 + (wide >> 4) - LOW, grid_y), x_here, reach)


def main_body(
    pivot, tiles, st_own, co_own, slots, keep, from_far, from_near,
    free, free_b, loads, loads_b, inverse, inverse_b, matrix, bands_z, bands_x,
    smoothed, filtered, uu, ss, vv, ub, sb, vb, st, co, res, inv, ratio, layers, out_f,
):
    odd = lax.axis_index("gy") % 2 == 1
    lane = iota((DEPTH, COLS), 1)

    def above(i):
        return jnp.where(odd, from_far[i].astype(F32), from_near[i].astype(F32))

    def below(i):
        return jnp.where(odd, from_near[i].astype(F32), from_far[i].astype(F32))

    def put(ref, row, fields):
        ref[pl.ds(row * 96, 48), :] = fields.astype(BF16)
        ref[pl.ds(row * 96 + 48, 48), :] = pltpu.roll(fields, COLS - 1, 1).astype(BF16)

    for row in range(17):
        n = row - LOW
        if n < 0:
            fields = [below(row * 3 + c) for c in range(3)]
            st[row] = below(12 + row)
            if n >= -2:
                co[row - 2] = below(14 + row)
        elif n < ROWS:
            fields = [tiles[n, c].astype(F32) for c in range(3)]
            st[row] = st_own[n]
            co[row - 2] = co_own[n]
        else:
            m = n - ROWS
            fields = [above(m * 3 + c) for c in range(3)]
            if m < 4:
                st[row] = above(15 + m)
            if m < 2:
                co[row - 2] = above(19 + m)
        put(uu, row, jnp.concatenate(fields, axis=0))

    def put_slots(ref, fields, beyond):
        after = pltpu.roll(fields, WIDE - 16, 1)
        if beyond is not None:
            last = iota(after.shape, 1) >= WIDE - 16
            after = jnp.where(last, beyond, after)
        for i, value in enumerate((fields, after)):
            ref[i * 96 : i * 96 + 48, :] = value.astype(BF16)
            ref[i * 96 + 48 : i * 96 + 96, :] = pltpu.roll(value, WIDE - 1, 1).astype(BF16)

    def side_by_side(p):
        up, mid, down = above(21 + p), slots[p].astype(F32), below(21 + p)
        joined = [jnp.where(lane < 64, down, mid), jnp.where(lane < 64, mid, up)]
        return jnp.concatenate(joined, axis=1), up

    pairs = [side_by_side(p) for p in range(5)]
    far_row = jnp.concatenate([up for _, up in pairs[:3]], axis=0)
    far_row = pltpu.roll(far_row, COLS - 16, 1)
    put_slots(
        ub,
        jnp.concatenate([f for f, _ in pairs[:3]], axis=0),
        jnp.concatenate([far_row, far_row], axis=1),
    )
    st_b, co_b = pairs[3][0], pairs[4][0]

    def product(x, stiff):
        f = jnp.dot(matrix[...], x, preferred_element_type=F32).reshape(2, 12, DEPTH, WIDE)
        g = f[0] * stiff[None] + f[1] * pltpu.roll(stiff, 1, 0)[None]
        return g.reshape(2, 2, 3 * DEPTH, WIDE)

    def two(ref, row):
        return jnp.concatenate(
            [ref[pl.ds(row * 96, 192), :], ref[pl.ds(row * 96 + 96, 192), :]], axis=1
        )

    def forces(ref, row, carry):
        g = product(two(ref, row), jnp.concatenate([st[row], st[row + 1]], axis=1))
        one = g[0, :, :, :COLS] + carry
        other = g[0, :, :, COLS:] + g[1, :, :, :COLS]
        return [h[0] + pltpu.roll(h[1], 1, 1) for h in (one, other)], g[1, :, :, COLS:]

    def forces_slots(x):
        g = product(x, st_b)
        h = g[0] + pltpu.roll(g[1].reshape(96, WIDE), 16, 1).reshape(2, 48, WIDE)
        return h[0] + pltpu.roll(h[1], 1, 1)

    def invert(both):
        diagonal = pivot * (both + pltpu.roll(both, 1, 1))
        some = diagonal > 0.0
        return jnp.where(some, 1.0 / jnp.where(some, diagonal, 1.0), 0.0)

    def step_of(residual, inverse_diagonal):
        step = (residual * (inverse_diagonal * (1.0 / spectral_mid))[None]).astype(BF16)
        return step.astype(F32).reshape(48, -1)

    def renew(old, step0, residual0, applied, mask, inverse_diagonal):
        width = mask.shape[-1]
        residual = residual0 - applied.reshape(3, DEPTH, width) * mask[None]
        step0 = step0.astype(F32).reshape(3, DEPTH, width)
        step1 = (second * first) * step0 + residual * (
            (2.0 * second / spectral_half) * inverse_diagonal
        )[None]
        new = old.astype(F32).reshape(3, DEPTH, width) + step0 + step1
        return new.astype(BF16).astype(F32).reshape(48, width)

    def first_pair(row, carry):
        before, weight = carry
        applied, after = forces(uu, row, before)
        for i in range(2):
            here = st[row + i] + pltpu.roll(st[row + i], 1, 0)
            inverse_diagonal = invert(here + weight)
            weight = here
            inv[row + i] = inverse_diagonal
            residual = loads[row + i] - applied[i].reshape(3, DEPTH, COLS)
            residual = residual * free[row + i][None]
            res[row + i] = residual
            put(ss, row + i, step_of(residual, inverse_diagonal))
        return after, weight

    zero = jnp.zeros((2, 48, COLS), F32)
    lax.fori_loop(
        0,
        8,
        lambda i, c: first_pair(2 * i, c),
        (zero, jnp.zeros((DEPTH, COLS), F32)),
        unroll=UNROLL[0],
    )
    here_b = st_b + pltpu.roll(st_b, 1, 0)
    inv_b = invert(here_b + pltpu.roll(here_b, 16, 1))
    res_b = (loads_b[...] - forces_slots(ub[...]).reshape(3, DEPTH, WIDE)) * free_b[...][None]
    put_slots(sb, step_of(res_b, inv_b), None)

    def second_pair(row, carry):
        applied, after = forces(ss, row, carry)
        for i in range(2):
            at = pl.ds((row + i) * 96, 48)
            new = renew(uu[at, :], ss[at, :], res[row + i], applied[i], free[row + i], inv[row + i])
            put(vv, row + i, new)
        return after

    lax.fori_loop(0, 7, lambda i, c: second_pair(2 * i + 1, c), zero, unroll=UNROLL[1])
    new_b = renew(ub[0:48, :], sb[0:48, :], res_b, forces_slots(sb[...]), free_b[...], inv_b)
    put_slots(vb, new_b, None)

    for y in range(ROWS):
        row, half = y + LOW, (y + LOW) // 8
        part = new_b[:, half * COLS : (half + 1) * COLS]
        part = pltpu.roll(part, (SLOT - 16 * (row % 8)) % COLS, 1)
        own = pltpu.roll(vv[row * 96 : row * 96 + 48, :].astype(F32), COLS - LOW, 1)
        own = jnp.where(iota((48, COLS), 1) <= SEAM, own, part)
        for c in range(3):
            out_f[pl.ds(c * 128 + y, DEPTH, stride=ROWS), :] = own[c * 16 : c * 16 + 16]
    smoothed[...] = out_f[...].astype(BF16)

    def energy(x):
        f = jnp.dot(matrix[...], x, preferred_element_type=F32).reshape(2, 12, DEPTH, WIDE)
        u = x.astype(F32).reshape(12, DEPTH, WIDE)
        over = jnp.sum(f[1] * u, axis=0)
        return jnp.sum(f[0] * u, axis=0) + pltpu.roll(over, DEPTH - 1, 0)

    def energy_pair(row, carry):
        value = energy(two(vv, row))
        for i in range(2):
            at = row + i - 2
            ratio[at, :, 0:COLS] = value[:, i * COLS : (i + 1) * COLS] * co[at] * inverse[at]
        return carry

    lax.fori_loop(0, 6, lambda i, c: energy_pair(2 * i + 2, c), 0, unroll=UNROLL[2])
    ratio_b = energy(vb[...]) * co_b * inverse_b[...]
    for at in range(12):
        row = at + 2
        part = ratio_b[:, (row // 8) * COLS : (row // 8 + 1) * COLS]
        ratio[at, :, COLS:WIDE] = pltpu.roll(part, (COLS - 16 * (row % 8)) % COLS, 1)

    for y in range(ROWS):
        a = jnp.concatenate(
            [ratio[y + 2], ratio[y + 1] + ratio[y + 3], ratio[y] + ratio[y + 4]], axis=0
        )
        s = jnp.dot(bands_z[...], a.astype(BF16), preferred_element_type=F32).astype(BF16)
        for k in range(6):
            layers[y * DEPTH : (y + 1) * DEPTH, k * WIDE : (k + 1) * WIDE] = s[
                k * DEPTH : (k + 1) * DEPTH
            ]
    total = jnp.dot(layers[...], bands_x[...], preferred_element_type=F32)
    for y in range(ROWS):
        filtered[pl.ds(y, DEPTH, stride=ROWS), :] = total[y * DEPTH : (y + 1) * DEPTH] * keep[y]


def main_scratch():
    return [
        pltpu.VMEM((17 * 96, COLS), BF16),
        pltpu.VMEM((16 * 96, COLS), BF16),
        pltpu.VMEM((15 * 96, COLS), BF16),
        pltpu.VMEM((192, WIDE), BF16),
        pltpu.VMEM((192, WIDE), BF16),
        pltpu.VMEM((192, WIDE), BF16),
        pltpu.VMEM((16, DEPTH, COLS), F32),
        pltpu.VMEM((12, DEPTH, COLS), F32),
        pltpu.VMEM((16, 3, DEPTH, COLS), F32),
        pltpu.VMEM((16, DEPTH, COLS), F32),
        pltpu.VMEM((12, DEPTH, WIDE), F32),
        pltpu.VMEM((128, 6 * WIDE), BF16),
        pltpu.VMEM((384, 128), F32),
    ]


def swapped(shard, axis, odd):
    size = lax.axis_size(axis)
    partner = [((i - odd) ^ 1) + odd for i in range(size)]
    return lax.ppermute(shard, axis, [(i, j) for i, j in enumerate(partner) if 0 <= j < size])


def shards(displacement, density, solid, fixed_nodes, load_nodes, load_forces):
    grid_y = ROWS * lax.axis_size("gy")
    grid_x = COLS * lax.axis_size("gx")
    table = stiffness_table()
    pivot = float(table[0, 0])
    tile = (DEPTH, COLS)

    given = (
        displacement.reshape(384, 128),
        density.reshape(128, 128),
        solid.reshape(128, 128),
    )
    um, st_own, co_own, keep, own, far, near = call(
        lambda *refs: pack_body(grid_y, grid_x, *refs),
        [
            shape_of((ROWS, 5) + tile, BF16),
            shape_of((ROWS,) + tile, F32),
            shape_of((ROWS,) + tile, F32),
            shape_of((ROWS,) + tile, F32),
            shape_of((5,) + tile, BF16),
            shape_of((5,) + tile, BF16),
            shape_of((5,) + tile, BF16),
        ],
        [pltpu.with_memory_space_constraint(array, pltpu.HBM) for array in given],
        [
            pltpu.VMEM((384, 128), BF16),
            pltpu.VMEM((128, 128), F32),
            pltpu.VMEM((128, 128), I32),
            pltpu.VMEM((384, 128), F32),
            pltpu.SemaphoreType.DMA((3,)),
        ],
        space=pltpu.HBM,
    )
    nodes, _ = lax.optimization_barrier((fixed_nodes, far))
    from_far = swapped(far, "gx", 1)
    from_near = swapped(near, "gx", 0)
    masks = call(
        lambda *refs: mask_body(grid_y, grid_x, *refs),
        [
            shape_of((16,) + tile, F32),
            shape_of((DEPTH, WIDE), F32),
            shape_of((16, 3) + tile, F32),
            shape_of((3, DEPTH, WIDE), F32),
            shape_of((12,) + tile, F32),
            shape_of((DEPTH, WIDE), F32),
        ],
        [nodes.reshape(1, -1), load_nodes.reshape(1, -1), load_forces.T],
        [pltpu.VMEM((256, WIDE), F32)],
        flops=2000000000,
    )
    from_far, from_near, masks = lax.optimization_barrier((from_far, from_near, masks))
    far, near, tiles, st, co, slots = call(
        merge_body,
        [
            shape_of((26,) + tile, BF16),
            shape_of((26,) + tile, BF16),
            shape_of((ROWS, 5) + tile, BF16),
            shape_of((ROWS,) + tile, F32),
            shape_of((ROWS,) + tile, F32),
            shape_of((5,) + tile, BF16),
        ],
        [um, st_own, co_own, own, from_far, from_near],
    )
    from_far = swapped(far, "gy", 1)
    from_near = swapped(near, "gy", 0)
    smoothed, filtered = call(
        lambda *refs: main_body(pivot, *refs),
        [shape_of((384, 128), BF16), shape_of((128, 128), F32)],
        [
            tiles,
            st,
            co,
            slots,
            keep,
            from_far,
            from_near,
            *masks,
            jnp.asarray(element_matrix(table), BF16),
            jnp.asarray(depth_bands(), BF16),
            jnp.asarray(along_bands(), BF16),
        ],
        main_scratch(),
        flops=10000000000,
    )
    return smoothed.reshape(3, DEPTH, ROWS, COLS), filtered.reshape(DEPTH, ROWS, COLS)


def solution(mesh):
    placed = (P(None, None, "gy", "gx"), P(None, "gy", "gx"), P(None, "gy", "gx"), P(), P(), P())
    return jax.shard_map(
        shards,
        mesh=mesh,
        in_specs=placed,
        out_specs=(P(None, None, "gy", "gx"), P(None, "gy", "gx")),
        check_vma=False,
    )
```

```python
import math

import jax
import jax.numpy as jnp
import numpy as np
from jax import lax
from jax.experimental import pallas as pl
from jax.experimental.pallas import tpu as pltpu
from jax.sharding import PartitionSpec as P

void_modulus = 0.001
spectral_mid = 1.375
spectral_half = 1.125
sigma = spectral_mid / spectral_half
first = 1.0 / sigma
second = 1.0 / (2.0 * sigma - first)

F32, BF16, I32 = jnp.float32, jnp.bfloat16, jnp.int32
DEPTH, ROWS, COLS = 16, 8, 128
LOW, HIGH = 4, 5
WIDE, SLOT, SEAM = 256, 117, 120
OWN = COLS - SLOT
PARTS = 2
UNROLL = (8, 7, 6)
KLASS = (0, 1, 2, 4, 5, 8)


def stiffness_table():
    poisson = 0.3
    lame = poisson / ((1.0 + poisson) * (1.0 - 2.0 * poisson))
    shear = 0.5 / (1.0 + poisson)
    elastic = np.zeros((6, 6))
    elastic[:3, :3] = lame
    for index in range(3):
        elastic[index, index] += 2.0 * shear
        elastic[index + 3, index + 3] = shear
    points = [0.5 - 0.5 / math.sqrt(3.0), 0.5 + 0.5 / math.sqrt(3.0)]
    table = np.zeros((24, 24))
    for point_z in points:
        for point_y in points:
            for point_x in points:
                strain = np.zeros((6, 24))
                for corner in range(8):
                    bit_z, bit_y, bit_x = (corner // 4, corner // 2 % 2, corner % 2)
                    shape_x = point_x if bit_x else 1.0 - point_x
                    shape_y = point_y if bit_y else 1.0 - point_y
                    shape_z = point_z if bit_z else 1.0 - point_z
                    slope_x = 1.0 if bit_x else -1.0
                    slope_y = 1.0 if bit_y else -1.0
                    slope_z = 1.0 if bit_z else -1.0
                    grad_x = slope_x * shape_y * shape_z
                    grad_y = shape_x * slope_y * shape_z
                    grad_z = shape_x * shape_y * slope_z
                    strain[0, corner] = grad_x
                    strain[1, 8 + corner] = grad_y
                    strain[2, 16 + corner] = grad_z
                    strain[3, corner] = grad_y
                    strain[3, 8 + corner] = grad_x
                    strain[4, 8 + corner] = grad_z
                    strain[4, 16 + corner] = grad_y
                    strain[5, corner] = grad_z
                    strain[5, 16 + corner] = grad_x
                table += strain.T @ elastic @ strain / 8.0
    return np.asarray(table.astype(np.float32).astype(jnp.bfloat16).astype(np.float64))


def element_matrix(table):
    matrix = np.zeros((2, 2, 2, 3, DEPTH, 2, 2, 3, DEPTH))
    for corner in range(8):
        bz, by, bx = corner // 4, corner // 2 % 2, corner % 2
        for other in range(8):
            oz, oy, ox = other // 4, other // 2 % 2, other % 2
            for c in range(3):
                for k in range(3):
                    for z in range(DEPTH - 1):
                        matrix[bz, by, bx, c, z + bz, oy, ox, k, z + oz] = table[
                            c * 8 + corner, k * 8 + other
                        ]
    return matrix.reshape(384, 192)


def depth_bands():
    bands = np.zeros((6, DEPTH, 3, DEPTH))
    for z in range(DEPTH):
        for dz in range(-2, 3):
            if 0 <= z + dz < DEPTH:
                for dy in range(3):
                    bands[KLASS.index(dz * dz + dy * dy), z, dy, z + dz] = 1.0
    return bands.reshape(96, 48)


def cone(square, dx):
    return max(0.0, 3.0 - math.sqrt(square + dx * dx))


def along_bands():
    bands = np.zeros((6, WIDE, COLS))
    for k, square in enumerate(KLASS):
        for x in range(COLS):
            for dx in range(-2, 3):
                at = x + dx
                lane = at + LOW if at <= SEAM else COLS + at - SLOT
                bands[k, lane, x] = cone(square, dx)
    return bands.reshape(6 * WIDE, COLS)


def iota(shape, dim):
    return lax.broadcasted_iota(I32, shape, dim)


def starts():
    return lax.axis_index("gy") * ROWS, lax.axis_index("gx") * COLS


def call(body, outs, ins, scratch=(), flops=0, limit=None, space=pltpu.VMEM):
    whole = pl.BlockSpec(memory_space=pltpu.VMEM)
    moved = sum(math.prod(o.shape) * o.dtype.itemsize for o in outs)
    return pl.pallas_call(
        body,
        out_shape=outs,
        in_specs=[pl.BlockSpec(memory_space=space)] * len(ins),
        out_specs=[whole] * len(outs),
        scratch_shapes=list(scratch),
        compiler_params=pltpu.CompilerParams(vmem_limit_bytes=limit or (32 << 20)),
        cost_estimate=pl.CostEstimate(flops=flops, bytes_accessed=moved, transcendentals=0),
    )(*ins)


def shape_of(shape, dtype):
    return jax.ShapeDtypeStruct(shape, dtype)


def slot_of(y):
    return 16 * ((y + LOW) % 8)


def weigh(grid_y, grid_x, inverse, inverse_b):
    y0, x0 = starts()
    lane = iota((DEPTH, COLS), 1)

    def within(pos, size):
        return jnp.where((pos >= 0) & (pos < size - 1), 1.0, 0.0)

    def along(xpos):
        ex = [within(xpos + d, grid_x) for d in range(-2, 3)]
        reach = {
            k: sum(cone(k, d) * ex[d + 2] for d in range(-2, 3) if cone(k, d) > 0.0)
            for k in KLASS
        }
        return ex[2], reach

    def around(pos, size):
        e = [within(pos + d, size) for d in range(-2, 3)]
        return e[2], e[1] + e[3], e[0] + e[4]

    def reciprocal(z_terms, y_terms, x_here, reach):
        total = 0.0
        for a in range(3):
            total = total + z_terms[a] * sum(y_terms[b] * reach[a * a + b * b] for b in range(3))
        alive = z_terms[0] * x_here * y_terms[0] > 0.0
        return jnp.where(alive, 1.0 / jnp.where(alive, total, 1.0), 0.0)

    x_here, reach = along(x0 + lane - LOW)
    z_terms = around(iota((DEPTH, COLS), 0), DEPTH)
    for row in range(12):
        inverse[row] = reciprocal(z_terms, around(y0 + row - 2, grid_y), x_here, reach)
    wide = iota((DEPTH, WIDE), 1)
    x_here, reach = along(x0 + SLOT + (wide & 15))
    z_terms = around(iota((DEPTH, WIDE), 0), DEPTH)
    inverse_b[...] = reciprocal(z_terms, around(y0 + (wide >> 4) - LOW, grid_y), x_here, reach)


def pack_body(
    grid_y, grid_x, u_in, den_in, sol_in, nodes_in,
    um, st_own, co_own, keep, own, far, near, inverse, inverse_b, nodes, u_ref, den_ref, sol_ref, uf, sem,
):
    copies = [
        pltpu.make_async_copy(source, target, sem.at[i])
        for i, (source, target) in enumerate(
            ((u_in, u_ref), (den_in, den_ref), (sol_in, sol_ref), (nodes_in, nodes))
        )
    ]
    for copy in copies:
        copy.start()
    y0, x0 = starts()
    odd = lax.axis_index("gx") % 2 == 1
    weigh(grid_y, grid_x, inverse, inverse_b)
    for copy in copies:
        copy.wait()
    uf[...] = u_ref[...].astype(F32)
    lane = iota((DEPTH, COLS), 1)
    inside_zx = (iota((DEPTH, COLS), 0) < DEPTH - 1) & (lane + x0 < grid_x - 1)
    blank = jnp.zeros((DEPTH, COLS), F32)
    middle, above, below = [blank] * 5, [blank] * 5, [blank] * 5
    for y in range(ROWS):
        planes = [uf[pl.ds(c * 128 + y, DEPTH, stride=ROWS), :] for c in range(3)]
        density = den_ref[pl.ds(y, DEPTH, stride=ROWS), :]
        solid = sol_ref[pl.ds(y, DEPTH, stride=ROWS), :]
        exists = inside_zx & (y0 + y < grid_y - 1)
        physical = jnp.where(solid == 1, 1.0, density)
        square = physical * physical
        stiff = jnp.where(exists, void_modulus + (1.0 - void_modulus) * (square * physical), 0.0)
        designed = (1 - solid).astype(F32)
        factor = jnp.where(exists, (-3.0 * (1.0 - void_modulus)) * square * designed, 0.0)
        keep[y] = jnp.where(exists, designed, 0.0)
        planes += [stiff, factor]
        st_own[y], co_own[y] = stiff, factor
        at = slot_of(y)
        for p, plane in enumerate(planes):
            if p < 3:
                um[y, p] = plane.astype(BF16)
            moved = pltpu.roll(plane, at + OWN, 1)
            middle[p] = jnp.where((lane >= at) & (lane < at + OWN), moved, middle[p])
            above[p] = jnp.where((lane >= at + OWN) & (lane < at + 16), moved, above[p])
            below[p] = jnp.where((lane >= at + OWN - LOW) & (lane < at + OWN), moved, below[p])
    for p in range(5):
        own[p] = middle[p].astype(BF16)
        far[p] = jnp.where(odd, below[p], above[p]).astype(BF16)
        near[p] = jnp.where(odd, above[p], below[p]).astype(BF16)


def merge_body(um, st_own, co_own, own, from_far, from_near, far, near, tiles, st, co, slots):
    odd_x = lax.axis_index("gx") % 2 == 1
    edge = iota((DEPTH, COLS), 1) < LOW
    for p in range(5):
        one, other = from_far[p].astype(F32), from_near[p].astype(F32)
        right, left = jnp.where(odd_x, one, other), jnp.where(odd_x, other, one)
        slots[p] = (own[p].astype(F32) + right).astype(BF16)
        for y in range(ROWS):
            rim = pltpu.roll(left, (COLS - slot_of(y) - OWN + LOW) % COLS, 1)
            tiles[y, p] = jnp.where(edge, rim, um[y, p].astype(F32)).astype(BF16)
            if p == 3:
                st[y] = jnp.where(edge, rim, st_own[y])
            if p == 4:
                co[y] = jnp.where(edge, rim, co_own[y])

    def fill(up, down):
        for y in range(HIGH):
            up[y * 3 : y * 3 + 3] = tiles[y, 0:3]
        up[15:19] = tiles[0:4, 3]
        up[19:21] = tiles[0:2, 4]
        up[21:26] = slots[...]
        for y in range(LOW):
            down[y * 3 : y * 3 + 3] = tiles[y + 4, 0:3]
        down[12:16] = tiles[4:8, 3]
        down[16:18] = tiles[6:8, 4]
        down[18:21] = jnp.zeros((3, DEPTH, COLS), BF16)
        down[21:26] = slots[...]

    odd = lax.axis_index("gy") % 2 == 1
    pl.when(odd)(lambda: fill(near, far))
    pl.when(jnp.logical_not(odd))(lambda: fill(far, near))


def one_hot(key, rows):
    return (iota((rows, key.shape[1]), 0) == key).astype(F32).astype(BF16)


def places(grid_y, grid_x, flat):
    y0, x0 = starts()
    x = (flat & (grid_x - 1)) - x0
    y = ((flat // grid_x) & (grid_y - 1)) - y0 + LOW
    z = flat // (grid_x * grid_y)
    slot = jnp.where((x >= SLOT) & (x < SLOT + 16), x - SLOT, -1)
    along = jnp.concatenate([one_hot(x + LOW, COLS), one_hot(slot, COLS)], axis=0)
    return along, y * DEPTH + z


def dots(a, b):
    return lax.dot_general(a, b, (((1,), (1,)), ((), ())), preferred_element_type=F32)


def split(total):
    lane = iota((DEPTH, COLS), 1)
    rows = total.reshape(16, DEPTH, WIDE)
    halves = [jnp.zeros((DEPTH, COLS), F32)] * 2
    for row in range(16):
        at = 16 * (row % 8)
        moved = pltpu.roll(rows[row, :, COLS:], at, 1)
        halves[row // 8] = jnp.where((lane >= at) & (lane < at + 16), moved, halves[row // 8])
    return rows[:, :, :COLS], jnp.concatenate(halves, axis=1)


def load_body(grid_y, grid_x, nodes, forces, um, st, co, loads, loads_b, tiles, st_own, co_own):
    for y in range(ROWS):
        planes = [um[y, c].astype(F32) for c in range(3)] + [st[y], co[y]]
        planes = [pltpu.roll(plane, LOW, 1) for plane in planes]
        for p, plane in enumerate(planes):
            tiles[y, p] = plane.astype(BF16)
        st_own[y], co_own[y] = planes[3:]
    at_x, ky = places(grid_y, grid_x, nodes[...])
    here = iota((256, ky.shape[1]), 0) == ky
    for c in range(3):
        force = forces[c : c + 1, :]
        total = jnp.zeros((256, WIDE), F32)
        for _ in range(PARTS):
            head = force.astype(BF16).astype(F32)
            total = total + dots(jnp.where(here, head, 0.0).astype(BF16), at_x)
            force = force - head
        loads[:, c], loads_b[c] = split(total)


def mask_body(grid_y, grid_x, fixed, free, free_b, spread):
    count = fixed.shape[1]
    part = 512
    spread[...] = jnp.zeros_like(spread)
    for at in range(0, count, part):
        kx, ky = places(grid_y, grid_x, fixed[:, at : at + part])
        spread[...] += dots(one_hot(ky, 256), kx)
    free[...], free_b[...] = split(jnp.where(spread[...] > 0.0, 0.0, 1.0))


def main_body(
    pivot, tiles, st_own, co_own, slots, keep, from_far, from_near,
    free, free_b, loads, loads_b, inverse, inverse_b, matrix, bands_z, bands_x,
    smoothed, filtered, uu, ss, vv, ub, sb, vb, st, co, res, inv, ratio, layers, out_f,
):
    odd = lax.axis_index("gy") % 2 == 1
    lane = iota((DEPTH, COLS), 1)

    def above(i):
        return jnp.where(odd, from_far[i].astype(F32), from_near[i].astype(F32))

    def below(i):
        return jnp.where(odd, from_near[i].astype(F32), from_far[i].astype(F32))

    def put(ref, row, fields):
        ref[pl.ds(row * 96, 48), :] = fields.astype(BF16)
        ref[pl.ds(row * 96 + 48, 48), :] = pltpu.roll(fields, COLS - 1, 1).astype(BF16)

    for row in range(17):
        n = row - LOW
        if n < 0:
            fields = [below(row * 3 + c) for c in range(3)]
            st[row] = below(12 + row)
            if n >= -2:
                co[row - 2] = below(14 + row)
        elif n < ROWS:
            fields = [tiles[n, c].astype(F32) for c in range(3)]
            st[row] = st_own[n]
            co[row - 2] = co_own[n]
        else:
            m = n - ROWS
            fields = [above(m * 3 + c) for c in range(3)]
            if m < 4:
                st[row] = above(15 + m)
            if m < 2:
                co[row - 2] = above(19 + m)
        put(uu, row, jnp.concatenate(fields, axis=0))

    def put_slots(ref, fields, beyond):
        after = pltpu.roll(fields, WIDE - 16, 1)
        if beyond is not None:
            last = iota(after.shape, 1) >= WIDE - 16
            after = jnp.where(last, beyond, after)
        for i, value in enumerate((fields, after)):
            ref[i * 96 : i * 96 + 48, :] = value.astype(BF16)
            ref[i * 96 + 48 : i * 96 + 96, :] = pltpu.roll(value, WIDE - 1, 1).astype(BF16)

    def side_by_side(p):
        up, mid, down = above(21 + p), slots[p].astype(F32), below(21 + p)
        joined = [jnp.where(lane < 64, down, mid), jnp.where(lane < 64, mid, up)]
        return jnp.concatenate(joined, axis=1), up

    pairs = [side_by_side(p) for p in range(5)]
    far_row = jnp.concatenate([up for _, up in pairs[:3]], axis=0)
    far_row = pltpu.roll(far_row, COLS - 16, 1)
    put_slots(
        ub,
        jnp.concatenate([f for f, _ in pairs[:3]], axis=0),
        jnp.concatenate([far_row, far_row], axis=1),
    )
    st_b, co_b = pairs[3][0], pairs[4][0]

    def product(x, stiff):
        f = jnp.dot(matrix[...], x, preferred_element_type=F32).reshape(2, 12, DEPTH, WIDE)
        g = f[0] * stiff[None] + f[1] * pltpu.roll(stiff, 1, 0)[None]
        return g.reshape(2, 2, 3 * DEPTH, WIDE)

    def two(ref, row):
        return jnp.concatenate(
            [ref[pl.ds(row * 96, 192), :], ref[pl.ds(row * 96 + 96, 192), :]], axis=1
        )

    def forces(ref, row, carry):
        g = product(two(ref, row), jnp.concatenate([st[row], st[row + 1]], axis=1))
        one = g[0, :, :, :COLS] + carry
        other = g[0, :, :, COLS:] + g[1, :, :, :COLS]
        return [h[0] + pltpu.roll(h[1], 1, 1) for h in (one, other)], g[1, :, :, COLS:]

    def forces_slots(x):
        g = product(x, st_b)
        h = g[0] + pltpu.roll(g[1].reshape(96, WIDE), 16, 1).reshape(2, 48, WIDE)
        return h[0] + pltpu.roll(h[1], 1, 1)

    def invert(both):
        diagonal = pivot * (both + pltpu.roll(both, 1, 1))
        some = diagonal > 0.0
        return jnp.where(some, 1.0 / jnp.where(some, diagonal, 1.0), 0.0)

    def step_of(residual, inverse_diagonal):
        step = (residual * (inverse_diagonal * (1.0 / spectral_mid))[None]).astype(BF16)
        return step.astype(F32).reshape(48, -1)

    def renew(old, step0, residual0, applied, mask, inverse_diagonal):
        width = mask.shape[-1]
        residual = residual0 - applied.reshape(3, DEPTH, width) * mask[None]
        step0 = step0.astype(F32).reshape(3, DEPTH, width)
        step1 = (second * first) * step0 + residual * (
            (2.0 * second / spectral_half) * inverse_diagonal
        )[None]
        new = old.astype(F32).reshape(3, DEPTH, width) + step0 + step1
        return new.astype(BF16).astype(F32).reshape(48, width)

    def first_pair(row, carry):
        before, weight = carry
        applied, after = forces(uu, row, before)
        for i in range(2):
            here = st[row + i] + pltpu.roll(st[row + i], 1, 0)
            inverse_diagonal = invert(here + weight)
            weight = here
            inv[row + i] = inverse_diagonal
            residual = loads[row + i] - applied[i].reshape(3, DEPTH, COLS)
            residual = residual * free[row + i][None]
            res[row + i] = residual
            put(ss, row + i, step_of(residual, inverse_diagonal))
        return after, weight

    zero = jnp.zeros((2, 48, COLS), F32)
    lax.fori_loop(
        0,
        8,
        lambda i, c: first_pair(2 * i, c),
        (zero, jnp.zeros((DEPTH, COLS), F32)),
        unroll=UNROLL[0],
    )
    here_b = st_b + pltpu.roll(st_b, 1, 0)
    inv_b = invert(here_b + pltpu.roll(here_b, 16, 1))
    res_b = (loads_b[...] - forces_slots(ub[...]).reshape(3, DEPTH, WIDE)) * free_b[...][None]
    put_slots(sb, step_of(res_b, inv_b), None)

    def second_pair(row, carry):
        applied, after = forces(ss, row, carry)
        for i in range(2):
            at = pl.ds((row + i) * 96, 48)
            new = renew(uu[at, :], ss[at, :], res[row + i], applied[i], free[row + i], inv[row + i])
            put(vv, row + i, new)
        return after

    lax.fori_loop(0, 7, lambda i, c: second_pair(2 * i + 1, c), zero, unroll=UNROLL[1])
    new_b = renew(ub[0:48, :], sb[0:48, :], res_b, forces_slots(sb[...]), free_b[...], inv_b)
    put_slots(vb, new_b, None)

    for y in range(ROWS):
        row, half = y + LOW, (y + LOW) // 8
        part = new_b[:, half * COLS : (half + 1) * COLS]
        part = pltpu.roll(part, (SLOT - 16 * (row % 8)) % COLS, 1)
        own = pltpu.roll(vv[row * 96 : row * 96 + 48, :].astype(F32), COLS - LOW, 1)
        own = jnp.where(iota((48, COLS), 1) <= SEAM, own, part)
        for c in range(3):
            out_f[pl.ds(c * 128 + y, DEPTH, stride=ROWS), :] = own[c * 16 : c * 16 + 16]
    smoothed[...] = out_f[...].astype(BF16)

    def energy(x):
        f = jnp.dot(matrix[...], x, preferred_element_type=F32).reshape(2, 12, DEPTH, WIDE)
        u = x.astype(F32).reshape(12, DEPTH, WIDE)
        over = jnp.sum(f[1] * u, axis=0)
        return jnp.sum(f[0] * u, axis=0) + pltpu.roll(over, DEPTH - 1, 0)

    def energy_pair(row, carry):
        value = energy(two(vv, row))
        for i in range(2):
            at = row + i - 2
            ratio[at, :, 0:COLS] = value[:, i * COLS : (i + 1) * COLS] * co[at] * inverse[at]
        return carry

    lax.fori_loop(0, 6, lambda i, c: energy_pair(2 * i + 2, c), 0, unroll=UNROLL[2])
    ratio_b = energy(vb[...]) * co_b * inverse_b[...]
    for at in range(12):
        row = at + 2
        part = ratio_b[:, (row // 8) * COLS : (row // 8 + 1) * COLS]
        ratio[at, :, COLS:WIDE] = pltpu.roll(part, (COLS - 16 * (row % 8)) % COLS, 1)

    for y in range(ROWS):
        a = jnp.concatenate(
            [ratio[y + 2], ratio[y + 1] + ratio[y + 3], ratio[y] + ratio[y + 4]], axis=0
        )
        s = jnp.dot(bands_z[...], a.astype(BF16), preferred_element_type=F32).astype(BF16)
        for k in range(6):
            layers[y * DEPTH : (y + 1) * DEPTH, k * WIDE : (k + 1) * WIDE] = s[
                k * DEPTH : (k + 1) * DEPTH
            ]
    total = jnp.dot(layers[...], bands_x[...], preferred_element_type=F32)
    for y in range(ROWS):
        filtered[pl.ds(y, DEPTH, stride=ROWS), :] = total[y * DEPTH : (y + 1) * DEPTH] * keep[y]


def main_scratch():
    return [
        pltpu.VMEM((17 * 96, COLS), BF16),
        pltpu.VMEM((16 * 96, COLS), BF16),
        pltpu.VMEM((15 * 96, COLS), BF16),
        pltpu.VMEM((192, WIDE), BF16),
        pltpu.VMEM((192, WIDE), BF16),
        pltpu.VMEM((192, WIDE), BF16),
        pltpu.VMEM((16, DEPTH, COLS), F32),
        pltpu.VMEM((12, DEPTH, COLS), F32),
        pltpu.VMEM((16, 3, DEPTH, COLS), F32),
        pltpu.VMEM((16, DEPTH, COLS), F32),
        pltpu.VMEM((12, DEPTH, WIDE), F32),
        pltpu.VMEM((128, 6 * WIDE), BF16),
        pltpu.VMEM((384, 128), F32),
    ]


def swapped(shard, axis, odd):
    size = lax.axis_size(axis)
    partner = [((i - odd) ^ 1) + odd for i in range(size)]
    return lax.ppermute(shard, axis, [(i, j) for i, j in enumerate(partner) if 0 <= j < size])


def shards(displacement, density, solid, fixed_nodes, load_nodes, load_forces):
    grid_y = ROWS * lax.axis_size("gy")
    grid_x = COLS * lax.axis_size("gx")
    table = stiffness_table()
    pivot = float(table[0, 0])
    tile = (DEPTH, COLS)

    given = (
        displacement.reshape(384, 128),
        density.reshape(128, 128),
        solid.reshape(128, 128),
        load_nodes.reshape(1, -1),
    )
    um, st, co, keep, own, far, near, inverse, inverse_b, nodes = call(
        lambda *refs: pack_body(grid_y, grid_x, *refs),
        [
            shape_of((ROWS, 3) + tile, BF16),
            shape_of((ROWS,) + tile, F32),
            shape_of((ROWS,) + tile, F32),
            shape_of((ROWS,) + tile, F32),
            shape_of((5,) + tile, BF16),
            shape_of((5,) + tile, BF16),
            shape_of((5,) + tile, BF16),
            shape_of((12,) + tile, F32),
            shape_of((DEPTH, WIDE), F32),
            shape_of((1, load_nodes.shape[0]), I32),
        ],
        [pltpu.with_memory_space_constraint(array, pltpu.HBM) for array in given],
        [
            pltpu.VMEM((384, 128), BF16),
            pltpu.VMEM((128, 128), F32),
            pltpu.VMEM((128, 128), I32),
            pltpu.VMEM((384, 128), F32),
            pltpu.SemaphoreType.DMA((4,)),
        ],
        space=pltpu.HBM,
    )
    st, _ = lax.optimization_barrier((st, near))
    from_far = swapped(far, "gx", 1)
    from_near = swapped(near, "gx", 0)
    *loads, um, st, co = call(
        lambda *refs: load_body(grid_y, grid_x, *refs),
        [
            shape_of((16, 3) + tile, F32),
            shape_of((3, DEPTH, WIDE), F32),
            shape_of((ROWS, 5) + tile, BF16),
            shape_of((ROWS,) + tile, F32),
            shape_of((ROWS,) + tile, F32),
        ],
        [nodes, load_forces.T, um, st, co],
        flops=1000000000,
    )
    from_far, from_near, um = lax.optimization_barrier((from_far, from_near, um))
    far, near, tiles, st, co, slots = call(
        merge_body,
        [
            shape_of((26,) + tile, BF16),
            shape_of((26,) + tile, BF16),
            shape_of((ROWS, 5) + tile, BF16),
            shape_of((ROWS,) + tile, F32),
            shape_of((ROWS,) + tile, F32),
            shape_of((5,) + tile, BF16),
        ],
        [um, st, co, own, from_far, from_near],
    )
    fixed, _ = lax.optimization_barrier((fixed_nodes, near))
    from_far = swapped(far, "gy", 1)
    from_near = swapped(near, "gy", 0)
    free, free_b = call(
        lambda *refs: mask_body(grid_y, grid_x, *refs),
        [
            shape_of((16,) + tile, F32),
            shape_of((DEPTH, WIDE), F32),
        ],
        [fixed.reshape(1, -1)],
        [pltpu.VMEM((256, WIDE), F32)],
        flops=1000000000,
    )
    smoothed, filtered = call(
        lambda *refs: main_body(pivot, *refs),
        [shape_of((384, 128), BF16), shape_of((128, 128), F32)],
        [
            tiles,
            st,
            co,
            slots,
            keep,
            from_far,
            from_near,
            free,
            free_b,
            *loads,
            inverse,
            inverse_b,
            jnp.asarray(element_matrix(table), BF16),
            jnp.asarray(depth_bands(), BF16),
            jnp.asarray(along_bands(), BF16),
        ],
        main_scratch(),
        flops=10000000000,
    )
    return smoothed.reshape(3, DEPTH, ROWS, COLS), filtered.reshape(DEPTH, ROWS, COLS)


def solution(mesh):
    placed = (P(None, None, "gy", "gx"), P(None, "gy", "gx"), P(None, "gy", "gx"), P(), P(), P())
    return jax.shard_map(
        shards,
        mesh=mesh,
        in_specs=placed,
        out_specs=(P(None, None, "gy", "gx"), P(None, "gy", "gx")),
        check_vma=False,
    )
```

```python
import math

import jax
import jax.numpy as jnp
import numpy as np
from jax import lax
from jax.experimental import pallas as pl
from jax.experimental.pallas import tpu as pltpu
from jax.sharding import PartitionSpec as P

void_modulus = 0.001
spectral_mid = 1.375
spectral_half = 1.125
sigma = spectral_mid / spectral_half
first = 1.0 / sigma
second = 1.0 / (2.0 * sigma - first)

F32, BF16, I32 = jnp.float32, jnp.bfloat16, jnp.int32
DEPTH, ROWS, COLS = 16, 8, 128
LOW, HIGH = 4, 5
WIDE, SLOT, SEAM = 256, 117, 120
OWN = COLS - SLOT
PARTS = 2
LAG, AT, LAST = (8, 15), (3, 11, 18), 21
KLASS = (0, 1, 2, 4, 5, 8)


def stiffness_table():
    poisson = 0.3
    lame = poisson / ((1.0 + poisson) * (1.0 - 2.0 * poisson))
    shear = 0.5 / (1.0 + poisson)
    elastic = np.zeros((6, 6))
    elastic[:3, :3] = lame
    for index in range(3):
        elastic[index, index] += 2.0 * shear
        elastic[index + 3, index + 3] = shear
    points = [0.5 - 0.5 / math.sqrt(3.0), 0.5 + 0.5 / math.sqrt(3.0)]
    table = np.zeros((24, 24))
    for point_z in points:
        for point_y in points:
            for point_x in points:
                strain = np.zeros((6, 24))
                for corner in range(8):
                    bit_z, bit_y, bit_x = (corner // 4, corner // 2 % 2, corner % 2)
                    shape_x = point_x if bit_x else 1.0 - point_x
                    shape_y = point_y if bit_y else 1.0 - point_y
                    shape_z = point_z if bit_z else 1.0 - point_z
                    slope_x = 1.0 if bit_x else -1.0
                    slope_y = 1.0 if bit_y else -1.0
                    slope_z = 1.0 if bit_z else -1.0
                    grad_x = slope_x * shape_y * shape_z
                    grad_y = shape_x * slope_y * shape_z
                    grad_z = shape_x * shape_y * slope_z
                    strain[0, corner] = grad_x
                    strain[1, 8 + corner] = grad_y
                    strain[2, 16 + corner] = grad_z
                    strain[3, corner] = grad_y
                    strain[3, 8 + corner] = grad_x
                    strain[4, 8 + corner] = grad_z
                    strain[4, 16 + corner] = grad_y
                    strain[5, corner] = grad_z
                    strain[5, 16 + corner] = grad_x
                table += strain.T @ elastic @ strain / 8.0
    return np.asarray(table.astype(np.float32).astype(jnp.bfloat16).astype(np.float64))


def element_matrix(table):
    matrix = np.zeros((2, 2, 2, 3, DEPTH, 2, 2, 3, DEPTH))
    for corner in range(8):
        bz, by, bx = corner // 4, corner // 2 % 2, corner % 2
        for other in range(8):
            oz, oy, ox = other // 4, other // 2 % 2, other % 2
            for c in range(3):
                for k in range(3):
                    for z in range(DEPTH - 1):
                        matrix[bz, by, bx, c, z + bz, oy, ox, k, z + oz] = table[
                            c * 8 + corner, k * 8 + other
                        ]
    return matrix.reshape(384, 192)


def depth_bands():
    bands = np.zeros((6, DEPTH, 3, DEPTH))
    for z in range(DEPTH):
        for dz in range(-2, 3):
            if 0 <= z + dz < DEPTH:
                for dy in range(3):
                    bands[KLASS.index(dz * dz + dy * dy), z, dy, z + dz] = 1.0
    return bands.reshape(96, 48)


def cone(square, dx):
    return max(0.0, 3.0 - math.sqrt(square + dx * dx))


def along_bands():
    bands = np.zeros((6, WIDE, COLS))
    for k, square in enumerate(KLASS):
        for x in range(COLS):
            for dx in range(-2, 3):
                at = x + dx
                lane = at + LOW if at <= SEAM else COLS + at - SLOT
                bands[k, lane, x] = cone(square, dx)
    return bands.reshape(6 * WIDE, COLS)


def iota(shape, dim):
    return lax.broadcasted_iota(I32, shape, dim)


def starts():
    return lax.axis_index("gy") * ROWS, lax.axis_index("gx") * COLS


def call(body, outs, ins, scratch=(), flops=0, limit=None, space=pltpu.VMEM):
    whole = pl.BlockSpec(memory_space=pltpu.VMEM)
    moved = sum(math.prod(o.shape) * o.dtype.itemsize for o in outs)
    return pl.pallas_call(
        body,
        out_shape=outs,
        in_specs=[pl.BlockSpec(memory_space=space)] * len(ins),
        out_specs=[whole] * len(outs),
        scratch_shapes=list(scratch),
        compiler_params=pltpu.CompilerParams(vmem_limit_bytes=limit or (32 << 20)),
        cost_estimate=pl.CostEstimate(flops=flops, bytes_accessed=moved, transcendentals=0),
    )(*ins)


def shape_of(shape, dtype):
    return jax.ShapeDtypeStruct(shape, dtype)


def slot_of(y):
    return 16 * ((y + LOW) % 8)


def weigh(grid_y, grid_x, inverse, inverse_b):
    y0, x0 = starts()
    lane = iota((DEPTH, COLS), 1)

    def within(pos, size):
        return jnp.where((pos >= 0) & (pos < size - 1), 1.0, 0.0)

    def along(xpos):
        ex = [within(xpos + d, grid_x) for d in range(-2, 3)]
        reach = {
            k: sum(cone(k, d) * ex[d + 2] for d in range(-2, 3) if cone(k, d) > 0.0)
            for k in KLASS
        }
        return ex[2], reach

    def around(pos, size):
        e = [within(pos + d, size) for d in range(-2, 3)]
        return e[2], e[1] + e[3], e[0] + e[4]

    def reciprocal(z_terms, y_terms, x_here, reach):
        total = 0.0
        for a in range(3):
            total = total + z_terms[a] * sum(y_terms[b] * reach[a * a + b * b] for b in range(3))
        alive = z_terms[0] * x_here * y_terms[0] > 0.0
        return jnp.where(alive, 1.0 / jnp.where(alive, total, 1.0), 0.0)

    x_here, reach = along(x0 + lane - LOW)
    z_terms = around(iota((DEPTH, COLS), 0), DEPTH)
    for row in range(12):
        inverse[row] = reciprocal(z_terms, around(y0 + row - 2, grid_y), x_here, reach)
    wide = iota((DEPTH, WIDE), 1)
    x_here, reach = along(x0 + SLOT + (wide & 15))
    z_terms = around(iota((DEPTH, WIDE), 0), DEPTH)
    inverse_b[...] = reciprocal(z_terms, around(y0 + (wide >> 4) - LOW, grid_y), x_here, reach)


def pack_body(
    grid_y, grid_x, u_in, den_in, sol_in, nodes_in,
    um, st_own, co_own, keep, own, far, near, inverse, inverse_b, nodes, u_ref, den_ref, sol_ref, uf, sem,
):
    copies = [
        pltpu.make_async_copy(source, target, sem.at[i])
        for i, (source, target) in enumerate(
            ((u_in, u_ref), (den_in, den_ref), (sol_in, sol_ref), (nodes_in, nodes))
        )
    ]
    for copy in copies:
        copy.start()
    y0, x0 = starts()
    odd = lax.axis_index("gx") % 2 == 1
    weigh(grid_y, grid_x, inverse, inverse_b)
    for copy in copies:
        copy.wait()
    uf[...] = u_ref[...].astype(F32)
    lane = iota((DEPTH, COLS), 1)
    inside_zx = (iota((DEPTH, COLS), 0) < DEPTH - 1) & (lane + x0 < grid_x - 1)
    blank = jnp.zeros((DEPTH, COLS), F32)
    middle, above, below = [blank] * 5, [blank] * 5, [blank] * 5
    for y in range(ROWS):
        planes = [uf[pl.ds(c * 128 + y, DEPTH, stride=ROWS), :] for c in range(3)]
        density = den_ref[pl.ds(y, DEPTH, stride=ROWS), :]
        solid = sol_ref[pl.ds(y, DEPTH, stride=ROWS), :]
        exists = inside_zx & (y0 + y < grid_y - 1)
        physical = jnp.where(solid == 1, 1.0, density)
        square = physical * physical
        stiff = jnp.where(exists, void_modulus + (1.0 - void_modulus) * (square * physical), 0.0)
        designed = (1 - solid).astype(F32)
        factor = jnp.where(exists, (-3.0 * (1.0 - void_modulus)) * square * designed, 0.0)
        keep[y] = jnp.where(exists, designed, 0.0)
        planes += [stiff, factor]
        st_own[y], co_own[y] = stiff, factor
        at = slot_of(y)
        for p, plane in enumerate(planes):
            if p < 3:
                um[y, p] = plane.astype(BF16)
            moved = pltpu.roll(plane, at + OWN, 1)
            middle[p] = jnp.where((lane >= at) & (lane < at + OWN), moved, middle[p])
            above[p] = jnp.where((lane >= at + OWN) & (lane < at + 16), moved, above[p])
            below[p] = jnp.where((lane >= at + OWN - LOW) & (lane < at + OWN), moved, below[p])
    for p in range(5):
        own[p] = middle[p].astype(BF16)
        far[p] = jnp.where(odd, below[p], above[p]).astype(BF16)
        near[p] = jnp.where(odd, above[p], below[p]).astype(BF16)


def merge_body(um, st_own, co_own, own, from_far, from_near, far, near, tiles, st, co, slots):
    odd_x = lax.axis_index("gx") % 2 == 1
    edge = iota((DEPTH, COLS), 1) < LOW
    for p in range(5):
        one, other = from_far[p].astype(F32), from_near[p].astype(F32)
        right, left = jnp.where(odd_x, one, other), jnp.where(odd_x, other, one)
        slots[p] = (own[p].astype(F32) + right).astype(BF16)
        for y in range(ROWS):
            rim = pltpu.roll(left, (COLS - slot_of(y) - OWN + LOW) % COLS, 1)
            tiles[y, p] = jnp.where(edge, rim, um[y, p].astype(F32)).astype(BF16)
            if p == 3:
                st[y] = jnp.where(edge, rim, st_own[y])
            if p == 4:
                co[y] = jnp.where(edge, rim, co_own[y])

    def fill(up, down):
        for y in range(HIGH):
            up[y * 3 : y * 3 + 3] = tiles[y, 0:3]
        up[15:19] = tiles[0:4, 3]
        up[19:21] = tiles[0:2, 4]
        up[21:26] = slots[...]
        for y in range(LOW):
            down[y * 3 : y * 3 + 3] = tiles[y + 4, 0:3]
        down[12:16] = tiles[4:8, 3]
        down[16:18] = tiles[6:8, 4]
        down[18:21] = jnp.zeros((3, DEPTH, COLS), BF16)
        down[21:26] = slots[...]

    odd = lax.axis_index("gy") % 2 == 1
    pl.when(odd)(lambda: fill(near, far))
    pl.when(jnp.logical_not(odd))(lambda: fill(far, near))


def one_hot(key, rows):
    return (iota((rows, key.shape[1]), 0) == key).astype(F32).astype(BF16)


def places(grid_y, grid_x, flat, slots):
    y0, x0 = starts()
    x = (flat & (grid_x - 1)) - x0
    y = ((flat // grid_x) & (grid_y - 1)) - y0 + LOW
    z = flat // (grid_x * grid_y)
    slot = jnp.where((x >= SLOT) & (x < SLOT + 16), x - SLOT, -1)
    along = jnp.concatenate([one_hot(x + LOW, COLS), one_hot(slot, slots)], axis=0)
    return along, y * DEPTH + z


def dots(a, b):
    return lax.dot_general(a, b, (((1,), (1,)), ((), ())), preferred_element_type=F32)


def split(total):
    lane = iota((DEPTH, COLS), 1)
    rows = total.reshape(16, DEPTH, WIDE)
    halves = [jnp.zeros((DEPTH, COLS), F32)] * 2
    for row in range(16):
        at = 16 * (row % 8)
        moved = pltpu.roll(rows[row, :, COLS:], at, 1)
        halves[row // 8] = jnp.where((lane >= at) & (lane < at + 16), moved, halves[row // 8])
    return rows[:, :, :COLS], jnp.concatenate(halves, axis=1)


def load_body(grid_y, grid_x, nodes, forces, um, st, co, loads, loads_b, tiles, st_own, co_own):
    for y in range(ROWS):
        planes = [um[y, c].astype(F32) for c in range(3)] + [st[y], co[y]]
        planes = [pltpu.roll(plane, LOW, 1) for plane in planes]
        for p, plane in enumerate(planes):
            tiles[y, p] = plane.astype(BF16)
        st_own[y], co_own[y] = planes[3:]
    at_x, ky = places(grid_y, grid_x, nodes[...], COLS)
    here = iota((256, ky.shape[1]), 0) == ky
    for c in range(3):
        force = forces[c : c + 1, :]
        total = jnp.zeros((256, WIDE), F32)
        for _ in range(PARTS):
            head = force.astype(BF16).astype(F32)
            total = total + dots(jnp.where(here, head, 0.0).astype(BF16), at_x)
            force = force - head
        loads[:, c], loads_b[c] = split(total)


def mask_body(grid_y, grid_x, fixed, free, free_b, spread):
    count = fixed.shape[1]
    part = 1024
    spread[...] = jnp.zeros_like(spread)
    for at in range(0, count, part):
        kx, ky = places(grid_y, grid_x, fixed[:, at : at + part], 16)
        spread[:, : COLS + 16] += dots(one_hot(ky, 256), kx)
    free[...], free_b[...] = split(jnp.where(spread[...] > 0.0, 0.0, 1.0))


def main_body(
    pivot, tiles, st_own, co_own, slots, keep, from_far, from_near,
    free, free_b, loads, loads_b, inverse, inverse_b, matrix, bands_z, bands_x,
    smoothed, filtered, uu, ss, vv, ub, sb, vb, st, co, res, inv, ratio, layers, out_f,
):
    odd = lax.axis_index("gy") % 2 == 1
    lane = iota((DEPTH, COLS), 1)

    def above(i):
        return jnp.where(odd, from_far[i].astype(F32), from_near[i].astype(F32))

    def below(i):
        return jnp.where(odd, from_near[i].astype(F32), from_far[i].astype(F32))

    def put(ref, row, fields):
        ref[pl.ds(row * 96, 48), :] = fields.astype(BF16)
        ref[pl.ds(row * 96 + 48, 48), :] = pltpu.roll(fields, COLS - 1, 1).astype(BF16)

    for row in range(17):
        n = row - LOW
        if n < 0:
            fields = [below(row * 3 + c) for c in range(3)]
            st[row] = below(12 + row)
            if n >= -2:
                co[row - 2] = below(14 + row)
        elif n < ROWS:
            fields = [tiles[n, c].astype(F32) for c in range(3)]
            st[row] = st_own[n]
            co[row - 2] = co_own[n]
        else:
            m = n - ROWS
            fields = [above(m * 3 + c) for c in range(3)]
            if m < 4:
                st[row] = above(15 + m)
            if m < 2:
                co[row - 2] = above(19 + m)
        put(uu, row, jnp.concatenate(fields, axis=0))

    def put_slots(ref, fields, beyond):
        after = pltpu.roll(fields, WIDE - 16, 1)
        if beyond is not None:
            last = iota(after.shape, 1) >= WIDE - 16
            after = jnp.where(last, beyond, after)
        for i, value in enumerate((fields, after)):
            ref[i * 96 : i * 96 + 48, :] = value.astype(BF16)
            ref[i * 96 + 48 : i * 96 + 96, :] = pltpu.roll(value, WIDE - 1, 1).astype(BF16)

    def side_by_side(p):
        up, mid, down = above(21 + p), slots[p].astype(F32), below(21 + p)
        joined = [jnp.where(lane < 64, down, mid), jnp.where(lane < 64, mid, up)]
        return jnp.concatenate(joined, axis=1), up

    pairs = [side_by_side(p) for p in range(5)]
    far_row = jnp.concatenate([up for _, up in pairs[:3]], axis=0)
    far_row = pltpu.roll(far_row, COLS - 16, 1)
    put_slots(
        ub,
        jnp.concatenate([f for f, _ in pairs[:3]], axis=0),
        jnp.concatenate([far_row, far_row], axis=1),
    )
    st_b, co_b = pairs[3][0], pairs[4][0]

    def product(x, stiff):
        f = jnp.dot(matrix[...], x, preferred_element_type=F32).reshape(2, 12, DEPTH, WIDE)
        g = f[0] * stiff[None] + f[1] * pltpu.roll(stiff, 1, 0)[None]
        return g.reshape(2, 2, 3 * DEPTH, WIDE)

    def two(ref, row):
        return jnp.concatenate(
            [ref[pl.ds(row * 96, 192), :], ref[pl.ds(row * 96 + 96, 192), :]], axis=1
        )

    def forces(ref, row, carry):
        g = product(two(ref, row), jnp.concatenate([st[row], st[row + 1]], axis=1))
        one = g[0, :, :, :COLS] + carry
        other = g[0, :, :, COLS:] + g[1, :, :, :COLS]
        return [h[0] + pltpu.roll(h[1], 1, 1) for h in (one, other)], g[1, :, :, COLS:]

    def forces_slots(x):
        g = product(x, st_b)
        h = g[0] + pltpu.roll(g[1].reshape(96, WIDE), 16, 1).reshape(2, 48, WIDE)
        return h[0] + pltpu.roll(h[1], 1, 1)

    def invert(both):
        diagonal = pivot * (both + pltpu.roll(both, 1, 1))
        some = diagonal > 0.0
        return jnp.where(some, 1.0 / jnp.where(some, diagonal, 1.0), 0.0)

    def step_of(residual, inverse_diagonal):
        step = (residual * (inverse_diagonal * (1.0 / spectral_mid))[None]).astype(BF16)
        return step.astype(F32).reshape(48, -1)

    def renew(old, step0, residual0, applied, mask, inverse_diagonal):
        width = mask.shape[-1]
        residual = residual0 - applied.reshape(3, DEPTH, width) * mask[None]
        step0 = step0.astype(F32).reshape(3, DEPTH, width)
        step1 = (second * first) * step0 + residual * (
            (2.0 * second / spectral_half) * inverse_diagonal
        )[None]
        new = old.astype(F32).reshape(3, DEPTH, width) + step0 + step1
        return new.astype(BF16).astype(F32).reshape(48, width)

    def first_pair(row, carry):
        before, weight = carry
        applied, after = forces(uu, row, before)
        for i in range(2):
            here = st[row + i] + pltpu.roll(st[row + i], 1, 0)
            inverse_diagonal = invert(here + weight)
            weight = here
            inv[row + i] = inverse_diagonal
            residual = loads[row + i] - applied[i].reshape(3, DEPTH, COLS)
            residual = residual * free[row + i][None]
            res[row + i] = residual
            put(ss, row + i, step_of(residual, inverse_diagonal))
        return after, weight

    zero = jnp.zeros((2, 48, COLS), F32)
    def second_pair(row, carry):
        applied, after = forces(ss, row, carry)
        for i in range(2):
            at = pl.ds((row + i) * 96, 48)
            new = renew(uu[at, :], ss[at, :], res[row + i], applied[i], free[row + i], inv[row + i])
            put(vv, row + i, new)
        return after

    def energy(x):
        f = jnp.dot(matrix[...], x, preferred_element_type=F32).reshape(2, 12, DEPTH, WIDE)
        u = x.astype(F32).reshape(12, DEPTH, WIDE)
        over = jnp.sum(f[1] * u, axis=0)
        return jnp.sum(f[0] * u, axis=0) + pltpu.roll(over, DEPTH - 1, 0)

    def energy_pair(row, carry):
        value = energy(two(vv, row))
        for i in range(2):
            at = row + i - 2
            ratio[at, :, 0:COLS] = value[:, i * COLS : (i + 1) * COLS] * co[at] * inverse[at]
        return carry

    carry, other_carry = (zero, jnp.zeros((DEPTH, COLS), F32)), zero
    for turn in range(LAST):
        if turn < 8:
            carry = first_pair(2 * turn, carry)
        if turn == AT[0]:
            here_b = st_b + pltpu.roll(st_b, 1, 0)
            inv_b = invert(here_b + pltpu.roll(here_b, 16, 1))
            res_b = (loads_b[...] - forces_slots(ub[...]).reshape(3, DEPTH, WIDE)) * free_b[...][None]
            put_slots(sb, step_of(res_b, inv_b), None)
        if 0 <= turn - LAG[0] < 7:
            other_carry = second_pair(2 * (turn - LAG[0]) + 1, other_carry)
        if turn == AT[1]:
            new_b = renew(ub[0:48, :], sb[0:48, :], res_b, forces_slots(sb[...]), free_b[...], inv_b)
            put_slots(vb, new_b, None)
        if 0 <= turn - LAG[1] < 6:
            energy_pair(2 * (turn - LAG[1]) + 2, 0)
        if turn == AT[2]:
            ratio_b = energy(vb[...]) * co_b * inverse_b[...]
    for at in range(12):
        row = at + 2
        part = ratio_b[:, (row // 8) * COLS : (row // 8 + 1) * COLS]
        ratio[at, :, COLS:WIDE] = pltpu.roll(part, (COLS - 16 * (row % 8)) % COLS, 1)

    for y in range(ROWS):
        row, half = y + LOW, (y + LOW) // 8
        part = new_b[:, half * COLS : (half + 1) * COLS]
        part = pltpu.roll(part, (SLOT - 16 * (row % 8)) % COLS, 1)
        own = pltpu.roll(vv[row * 96 : row * 96 + 48, :].astype(F32), COLS - LOW, 1)
        own = jnp.where(iota((48, COLS), 1) <= SEAM, own, part)
        for c in range(3):
            out_f[pl.ds(c * 128 + y, DEPTH, stride=ROWS), :] = own[c * 16 : c * 16 + 16]
    smoothed[...] = out_f[...].astype(BF16)

    for y in range(ROWS):
        a = jnp.concatenate(
            [ratio[y + 2], ratio[y + 1] + ratio[y + 3], ratio[y] + ratio[y + 4]], axis=0
        )
        s = jnp.dot(bands_z[...], a.astype(BF16), preferred_element_type=F32).astype(BF16)
        for k in range(6):
            layers[y * DEPTH : (y + 1) * DEPTH, k * WIDE : (k + 1) * WIDE] = s[
                k * DEPTH : (k + 1) * DEPTH
            ]
    total = jnp.dot(layers[...], bands_x[...], preferred_element_type=F32)
    for y in range(ROWS):
        filtered[pl.ds(y, DEPTH, stride=ROWS), :] = total[y * DEPTH : (y + 1) * DEPTH] * keep[y]


def main_scratch():
    return [
        pltpu.VMEM((17 * 96, COLS), BF16),
        pltpu.VMEM((16 * 96, COLS), BF16),
        pltpu.VMEM((15 * 96, COLS), BF16),
        pltpu.VMEM((192, WIDE), BF16),
        pltpu.VMEM((192, WIDE), BF16),
        pltpu.VMEM((192, WIDE), BF16),
        pltpu.VMEM((16, DEPTH, COLS), F32),
        pltpu.VMEM((12, DEPTH, COLS), F32),
        pltpu.VMEM((16, 3, DEPTH, COLS), F32),
        pltpu.VMEM((16, DEPTH, COLS), F32),
        pltpu.VMEM((12, DEPTH, WIDE), F32),
        pltpu.VMEM((128, 6 * WIDE), BF16),
        pltpu.VMEM((384, 128), F32),
    ]


def swapped(shard, axis, odd):
    size = lax.axis_size(axis)
    partner = [((i - odd) ^ 1) + odd for i in range(size)]
    return lax.ppermute(shard, axis, [(i, j) for i, j in enumerate(partner) if 0 <= j < size])


def shards(displacement, density, solid, fixed_nodes, load_nodes, load_forces):
    grid_y = ROWS * lax.axis_size("gy")
    grid_x = COLS * lax.axis_size("gx")
    table = stiffness_table()
    pivot = float(table[0, 0])
    tile = (DEPTH, COLS)

    given = (
        displacement.reshape(384, 128),
        density.reshape(128, 128),
        solid.reshape(128, 128),
        load_nodes.reshape(1, -1),
    )
    um, st, co, keep, own, far, near, inverse, inverse_b, nodes = call(
        lambda *refs: pack_body(grid_y, grid_x, *refs),
        [
            shape_of((ROWS, 3) + tile, BF16),
            shape_of((ROWS,) + tile, F32),
            shape_of((ROWS,) + tile, F32),
            shape_of((ROWS,) + tile, F32),
            shape_of((5,) + tile, BF16),
            shape_of((5,) + tile, BF16),
            shape_of((5,) + tile, BF16),
            shape_of((12,) + tile, F32),
            shape_of((DEPTH, WIDE), F32),
            shape_of((1, load_nodes.shape[0]), I32),
        ],
        [pltpu.with_memory_space_constraint(array, pltpu.HBM) for array in given],
        [
            pltpu.VMEM((384, 128), BF16),
            pltpu.VMEM((128, 128), F32),
            pltpu.VMEM((128, 128), I32),
            pltpu.VMEM((384, 128), F32),
            pltpu.SemaphoreType.DMA((4,)),
        ],
        space=pltpu.HBM,
    )
    st, _ = lax.optimization_barrier((st, near))
    from_far = swapped(far, "gx", 1)
    from_near = swapped(near, "gx", 0)
    *loads, um, st, co = call(
        lambda *refs: load_body(grid_y, grid_x, *refs),
        [
            shape_of((16, 3) + tile, F32),
            shape_of((3, DEPTH, WIDE), F32),
            shape_of((ROWS, 5) + tile, BF16),
            shape_of((ROWS,) + tile, F32),
            shape_of((ROWS,) + tile, F32),
        ],
        [nodes, load_forces.T, um, st, co],
        flops=1000000000,
    )
    from_far, from_near, um = lax.optimization_barrier((from_far, from_near, um))
    far, near, tiles, st, co, slots = call(
        merge_body,
        [
            shape_of((26,) + tile, BF16),
            shape_of((26,) + tile, BF16),
            shape_of((ROWS, 5) + tile, BF16),
            shape_of((ROWS,) + tile, F32),
            shape_of((ROWS,) + tile, F32),
            shape_of((5,) + tile, BF16),
        ],
        [um, st, co, own, from_far, from_near],
    )
    fixed, _ = lax.optimization_barrier((fixed_nodes, near))
    from_far = swapped(far, "gy", 1)
    from_near = swapped(near, "gy", 0)
    free, free_b = call(
        lambda *refs: mask_body(grid_y, grid_x, *refs),
        [
            shape_of((16,) + tile, F32),
            shape_of((DEPTH, WIDE), F32),
        ],
        [fixed.reshape(1, -1)],
        [pltpu.VMEM((256, WIDE), F32)],
        flops=1000000000,
    )
    smoothed, filtered = call(
        lambda *refs: main_body(pivot, *refs),
        [shape_of((384, 128), BF16), shape_of((128, 128), F32)],
        [
            tiles,
            st,
            co,
            slots,
            keep,
            from_far,
            from_near,
            free,
            free_b,
            *loads,
            inverse,
            inverse_b,
            jnp.asarray(element_matrix(table), BF16),
            jnp.asarray(depth_bands(), BF16),
            jnp.asarray(along_bands(), BF16),
        ],
        main_scratch(),
        flops=10000000000,
    )
    return smoothed.reshape(3, DEPTH, ROWS, COLS), filtered.reshape(DEPTH, ROWS, COLS)


def solution(mesh):
    placed = (P(None, None, "gy", "gx"), P(None, "gy", "gx"), P(None, "gy", "gx"), P(), P(), P())
    return jax.shard_map(
        shards,
        mesh=mesh,
        in_specs=placed,
        out_specs=(P(None, None, "gy", "gx"), P(None, "gy", "gx")),
        check_vma=False,
    )
```

```python
import math

import jax
import jax.numpy as jnp
import numpy as np
from jax import lax
from jax.experimental import pallas as pl
from jax.experimental.pallas import tpu as pltpu
from jax.sharding import PartitionSpec as P

void_modulus = 0.001
spectral_mid = 1.375
spectral_half = 1.125
sigma = spectral_mid / spectral_half
first = 1.0 / sigma
second = 1.0 / (2.0 * sigma - first)

F32, BF16, I32 = jnp.float32, jnp.bfloat16, jnp.int32
DEPTH, ROWS, COLS = 16, 8, 128
LOW, HIGH = 4, 5
WIDE, SLOT, SEAM = 256, 117, 120
OWN = COLS - SLOT
PARTS = 2
LAG, AT, LAST = (8, 15), (3, 11, 18), 21
KLASS = (0, 1, 2, 4, 5, 8)


def stiffness_table():
    poisson = 0.3
    lame = poisson / ((1.0 + poisson) * (1.0 - 2.0 * poisson))
    shear = 0.5 / (1.0 + poisson)
    elastic = np.zeros((6, 6))
    elastic[:3, :3] = lame
    for index in range(3):
        elastic[index, index] += 2.0 * shear
        elastic[index + 3, index + 3] = shear
    points = [0.5 - 0.5 / math.sqrt(3.0), 0.5 + 0.5 / math.sqrt(3.0)]
    table = np.zeros((24, 24))
    for point_z in points:
        for point_y in points:
            for point_x in points:
                strain = np.zeros((6, 24))
                for corner in range(8):
                    bit_z, bit_y, bit_x = (corner // 4, corner // 2 % 2, corner % 2)
                    shape_x = point_x if bit_x else 1.0 - point_x
                    shape_y = point_y if bit_y else 1.0 - point_y
                    shape_z = point_z if bit_z else 1.0 - point_z
                    slope_x = 1.0 if bit_x else -1.0
                    slope_y = 1.0 if bit_y else -1.0
                    slope_z = 1.0 if bit_z else -1.0
                    grad_x = slope_x * shape_y * shape_z
                    grad_y = shape_x * slope_y * shape_z
                    grad_z = shape_x * shape_y * slope_z
                    strain[0, corner] = grad_x
                    strain[1, 8 + corner] = grad_y
                    strain[2, 16 + corner] = grad_z
                    strain[3, corner] = grad_y
                    strain[3, 8 + corner] = grad_x
                    strain[4, 8 + corner] = grad_z
                    strain[4, 16 + corner] = grad_y
                    strain[5, corner] = grad_z
                    strain[5, 16 + corner] = grad_x
                table += strain.T @ elastic @ strain / 8.0
    return np.asarray(table.astype(np.float32).astype(jnp.bfloat16).astype(np.float64))


def element_matrix(table):
    matrix = np.zeros((2, 2, 2, 3, DEPTH, 2, 2, 3, DEPTH))
    for corner in range(8):
        bz, by, bx = corner // 4, corner // 2 % 2, corner % 2
        for other in range(8):
            oz, oy, ox = other // 4, other // 2 % 2, other % 2
            for c in range(3):
                for k in range(3):
                    for z in range(DEPTH - 1):
                        matrix[bz, by, bx, c, z + bz, oy, ox, k, z + oz] = table[
                            c * 8 + corner, k * 8 + other
                        ]
    return matrix.reshape(384, 192)


def depth_bands():
    bands = np.zeros((6, DEPTH, 3, DEPTH))
    for z in range(DEPTH):
        for dz in range(-2, 3):
            if 0 <= z + dz < DEPTH:
                for dy in range(3):
                    bands[KLASS.index(dz * dz + dy * dy), z, dy, z + dz] = 1.0
    return bands.reshape(96, 48)


def cone(square, dx):
    return max(0.0, 3.0 - math.sqrt(square + dx * dx))


def along_bands():
    bands = np.zeros((6, WIDE, COLS))
    for k, square in enumerate(KLASS):
        for x in range(COLS):
            for dx in range(-2, 3):
                at = x + dx
                lane = at + LOW if at <= SEAM else COLS + at - SLOT
                bands[k, lane, x] = cone(square, dx)
    return bands.reshape(6 * WIDE, COLS)


def iota(shape, dim):
    return lax.broadcasted_iota(I32, shape, dim)


def starts():
    return lax.axis_index("gy") * ROWS, lax.axis_index("gx") * COLS


def call(body, outs, ins, scratch=(), flops=0, limit=None, space=pltpu.VMEM):
    whole = pl.BlockSpec(memory_space=pltpu.VMEM)
    moved = sum(math.prod(o.shape) * o.dtype.itemsize for o in outs)
    return pl.pallas_call(
        body,
        out_shape=outs,
        in_specs=[pl.BlockSpec(memory_space=space)] * len(ins),
        out_specs=[whole] * len(outs),
        scratch_shapes=list(scratch),
        compiler_params=pltpu.CompilerParams(vmem_limit_bytes=limit or (32 << 20)),
        cost_estimate=pl.CostEstimate(flops=flops, bytes_accessed=moved, transcendentals=0),
    )(*ins)


def shape_of(shape, dtype):
    return jax.ShapeDtypeStruct(shape, dtype)


def slot_of(y):
    return 16 * ((y + LOW) % 8)


def weigh(grid_y, grid_x, inverse, inverse_b):
    y0, x0 = starts()
    lane = iota((DEPTH, COLS), 1)

    def within(pos, size):
        return jnp.where((pos >= 0) & (pos < size - 1), 1.0, 0.0)

    def along(xpos):
        ex = [within(xpos + d, grid_x) for d in range(-2, 3)]
        reach = {
            k: sum(cone(k, d) * ex[d + 2] for d in range(-2, 3) if cone(k, d) > 0.0)
            for k in KLASS
        }
        return ex[2], reach

    def around(pos, size):
        e = [within(pos + d, size) for d in range(-2, 3)]
        return e[2], e[1] + e[3], e[0] + e[4]

    def reciprocal(z_terms, y_terms, x_here, reach):
        total = 0.0
        for a in range(3):
            total = total + z_terms[a] * sum(y_terms[b] * reach[a * a + b * b] for b in range(3))
        alive = z_terms[0] * x_here * y_terms[0] > 0.0
        return jnp.where(alive, 1.0 / jnp.where(alive, total, 1.0), 0.0)

    x_here, reach = along(x0 + lane - LOW)
    z_terms = around(iota((DEPTH, COLS), 0), DEPTH)
    for row in range(12):
        inverse[row] = reciprocal(z_terms, around(y0 + row - 2, grid_y), x_here, reach)
    wide = iota((DEPTH, WIDE), 1)
    x_here, reach = along(x0 + SLOT + (wide & 15))
    z_terms = around(iota((DEPTH, WIDE), 0), DEPTH)
    inverse_b[...] = reciprocal(z_terms, around(y0 + (wide >> 4) - LOW, grid_y), x_here, reach)


def pack_body(
    grid_y, grid_x, u_in, den_in, sol_in, nodes_in,
    um, st_own, co_own, keep, own, far, near, inverse, inverse_b, nodes, u_ref, den_ref, sol_ref, uf, sem,
):
    copies = [
        pltpu.make_async_copy(source, target, sem.at[i])
        for i, (source, target) in enumerate(
            ((u_in, u_ref), (den_in, den_ref), (sol_in, sol_ref), (nodes_in, nodes))
        )
    ]
    for copy in copies:
        copy.start()
    y0, x0 = starts()
    odd = lax.axis_index("gx") % 2 == 1
    weigh(grid_y, grid_x, inverse, inverse_b)
    for copy in copies:
        copy.wait()
    uf[...] = u_ref[...].astype(F32)
    lane = iota((DEPTH, COLS), 1)
    inside_zx = (iota((DEPTH, COLS), 0) < DEPTH - 1) & (lane + x0 < grid_x - 1)
    blank = jnp.zeros((DEPTH, COLS), F32)
    middle, above, below = [blank] * 5, [blank] * 5, [blank] * 5
    for y in range(ROWS):
        planes = [uf[pl.ds(c * 128 + y, DEPTH, stride=ROWS), :] for c in range(3)]
        density = den_ref[pl.ds(y, DEPTH, stride=ROWS), :]
        solid = sol_ref[pl.ds(y, DEPTH, stride=ROWS), :]
        exists = inside_zx & (y0 + y < grid_y - 1)
        physical = jnp.where(solid == 1, 1.0, density)
        square = physical * physical
        stiff = jnp.where(exists, void_modulus + (1.0 - void_modulus) * (square * physical), 0.0)
        designed = (1 - solid).astype(F32)
        factor = jnp.where(exists, (-3.0 * (1.0 - void_modulus)) * square * designed, 0.0)
        keep[y] = jnp.where(exists, designed, 0.0)
        planes += [stiff, factor]
        st_own[y], co_own[y] = stiff, factor
        at = slot_of(y)
        for p, plane in enumerate(planes):
            if p < 3:
                um[y, p] = plane.astype(BF16)
            moved = pltpu.roll(plane, at + OWN, 1)
            middle[p] = jnp.where((lane >= at) & (lane < at + OWN), moved, middle[p])
            above[p] = jnp.where((lane >= at + OWN) & (lane < at + 16), moved, above[p])
            below[p] = jnp.where((lane >= at + OWN - LOW) & (lane < at + OWN), moved, below[p])
    for p in range(5):
        own[p] = middle[p].astype(BF16)
        far[p] = jnp.where(odd, below[p], above[p]).astype(BF16)
        near[p] = jnp.where(odd, above[p], below[p]).astype(BF16)


def merge_body(um, st_own, co_own, own, from_far, from_near, far, near, tiles, st, co, slots):
    odd_x = lax.axis_index("gx") % 2 == 1
    edge = iota((DEPTH, COLS), 1) < LOW
    for p in range(5):
        one, other = from_far[p].astype(F32), from_near[p].astype(F32)
        right, left = jnp.where(odd_x, one, other), jnp.where(odd_x, other, one)
        slots[p] = (own[p].astype(F32) + right).astype(BF16)
        for y in range(ROWS):
            rim = pltpu.roll(left, (COLS - slot_of(y) - OWN + LOW) % COLS, 1)
            tiles[y, p] = jnp.where(edge, rim, um[y, p].astype(F32)).astype(BF16)
            if p == 3:
                st[y] = jnp.where(edge, rim, st_own[y])
            if p == 4:
                co[y] = jnp.where(edge, rim, co_own[y])

    def fill(up, down):
        for y in range(HIGH):
            up[y * 3 : y * 3 + 3] = tiles[y, 0:3]
        up[15:19] = tiles[0:4, 3]
        up[19:21] = tiles[0:2, 4]
        up[21:26] = slots[...]
        for y in range(LOW):
            down[y * 3 : y * 3 + 3] = tiles[y + 4, 0:3]
        down[12:16] = tiles[4:8, 3]
        down[16:18] = tiles[6:8, 4]
        down[18:21] = jnp.zeros((3, DEPTH, COLS), BF16)
        down[21:26] = slots[...]

    odd = lax.axis_index("gy") % 2 == 1
    pl.when(odd)(lambda: fill(near, far))
    pl.when(jnp.logical_not(odd))(lambda: fill(far, near))


def one_hot(key, rows):
    return (iota((rows, key.shape[1]), 0) == key).astype(F32).astype(BF16)


def places(grid_y, grid_x, flat, slots):
    y0, x0 = starts()
    x = (flat & (grid_x - 1)) - x0
    y = ((flat // grid_x) & (grid_y - 1)) - y0 + LOW
    z = flat // (grid_x * grid_y)
    slot = jnp.where((x >= SLOT) & (x < SLOT + 16), x - SLOT, -1)
    along = jnp.concatenate([one_hot(x + LOW, COLS), one_hot(slot, slots)], axis=0)
    return along, y * DEPTH + z


def dots(a, b):
    return lax.dot_general(a, b, (((1,), (1,)), ((), ())), preferred_element_type=F32)


def split(total):
    lane = iota((DEPTH, COLS), 1)
    rows = total.reshape(16, DEPTH, WIDE)
    halves = [jnp.zeros((DEPTH, COLS), F32)] * 2
    for row in range(16):
        at = 16 * (row % 8)
        moved = pltpu.roll(rows[row, :, COLS:], at, 1)
        halves[row // 8] = jnp.where((lane >= at) & (lane < at + 16), moved, halves[row // 8])
    return rows[:, :, :COLS], jnp.concatenate(halves, axis=1)


def load_body(grid_y, grid_x, nodes, forces, um, st, co, loads, loads_b, tiles, st_own, co_own):
    for y in range(ROWS):
        planes = [um[y, c].astype(F32) for c in range(3)] + [st[y], co[y]]
        planes = [pltpu.roll(plane, LOW, 1) for plane in planes]
        for p, plane in enumerate(planes):
            tiles[y, p] = plane.astype(BF16)
        st_own[y], co_own[y] = planes[3:]
    at_x, ky = places(grid_y, grid_x, nodes[...], COLS)
    here = iota((256, ky.shape[1]), 0) == ky
    for c in range(3):
        force = forces[c : c + 1, :]
        total = jnp.zeros((256, WIDE), F32)
        for _ in range(PARTS):
            head = force.astype(BF16).astype(F32)
            total = total + dots(jnp.where(here, head, 0.0).astype(BF16), at_x)
            force = force - head
        loads[:, c], loads_b[c] = split(total)


def mask_body(grid_y, grid_x, fixed, free, free_b, spread):
    count = fixed.shape[1]
    part = 2048
    spread[...] = jnp.zeros_like(spread)
    for at in range(0, count, part):
        kx, ky = places(grid_y, grid_x, fixed[:, at : at + part], 16)
        spread[:, : COLS + 16] += dots(one_hot(ky, 256), kx)
    free[...], free_b[...] = split(jnp.where(spread[...] > 0.0, 0.0, 1.0))


def main_body(
    pivot, tiles, st_own, co_own, slots, keep, from_far, from_near,
    free, free_b, loads, loads_b, inverse, inverse_b, matrix, bands_z, bands_x,
    smoothed, filtered, uu, ss, vv, ub, sb, vb, st, co, res, inv, ratio, layers, out_f,
):
    odd = lax.axis_index("gy") % 2 == 1
    lane = iota((DEPTH, COLS), 1)

    def above(i):
        return jnp.where(odd, from_far[i].astype(F32), from_near[i].astype(F32))

    def below(i):
        return jnp.where(odd, from_near[i].astype(F32), from_far[i].astype(F32))

    def put(ref, row, fields):
        ref[pl.ds(row * 96, 48), :] = fields.astype(BF16)
        ref[pl.ds(row * 96 + 48, 48), :] = pltpu.roll(fields, COLS - 1, 1).astype(BF16)

    for row in range(17):
        n = row - LOW
        if n < 0:
            fields = [below(row * 3 + c) for c in range(3)]
            st[row] = below(12 + row)
            if n >= -2:
                co[row - 2] = below(14 + row)
        elif n < ROWS:
            fields = [tiles[n, c].astype(F32) for c in range(3)]
            st[row] = st_own[n]
            co[row - 2] = co_own[n]
        else:
            m = n - ROWS
            fields = [above(m * 3 + c) for c in range(3)]
            if m < 4:
                st[row] = above(15 + m)
            if m < 2:
                co[row - 2] = above(19 + m)
        put(uu, row, jnp.concatenate(fields, axis=0))

    def put_slots(ref, fields, beyond):
        after = pltpu.roll(fields, WIDE - 16, 1)
        if beyond is not None:
            last = iota(after.shape, 1) >= WIDE - 16
            after = jnp.where(last, beyond, after)
        for i, value in enumerate((fields, after)):
            ref[i * 96 : i * 96 + 48, :] = value.astype(BF16)
            ref[i * 96 + 48 : i * 96 + 96, :] = pltpu.roll(value, WIDE - 1, 1).astype(BF16)

    def side_by_side(p):
        up, mid, down = above(21 + p), slots[p].astype(F32), below(21 + p)
        joined = [jnp.where(lane < 64, down, mid), jnp.where(lane < 64, mid, up)]
        return jnp.concatenate(joined, axis=1), up

    pairs = [side_by_side(p) for p in range(5)]
    far_row = jnp.concatenate([up for _, up in pairs[:3]], axis=0)
    far_row = pltpu.roll(far_row, COLS - 16, 1)
    put_slots(
        ub,
        jnp.concatenate([f for f, _ in pairs[:3]], axis=0),
        jnp.concatenate([far_row, far_row], axis=1),
    )
    st_b, co_b = pairs[3][0], pairs[4][0]

    def product(x, stiff):
        f = jnp.dot(matrix[...], x, preferred_element_type=F32).reshape(2, 12, DEPTH, WIDE)
        g = f[0] * stiff[None] + f[1] * pltpu.roll(stiff, 1, 0)[None]
        return g.reshape(2, 2, 3 * DEPTH, WIDE)

    def two(ref, row):
        return jnp.concatenate(
            [ref[pl.ds(row * 96, 192), :], ref[pl.ds(row * 96 + 96, 192), :]], axis=1
        )

    def forces(ref, row, carry):
        g = product(two(ref, row), jnp.concatenate([st[row], st[row + 1]], axis=1))
        one = g[0, :, :, :COLS] + carry
        other = g[0, :, :, COLS:] + g[1, :, :, :COLS]
        return [h[0] + pltpu.roll(h[1], 1, 1) for h in (one, other)], g[1, :, :, COLS:]

    def forces_slots(x):
        g = product(x, st_b)
        h = g[0] + pltpu.roll(g[1].reshape(96, WIDE), 16, 1).reshape(2, 48, WIDE)
        return h[0] + pltpu.roll(h[1], 1, 1)

    def invert(both):
        diagonal = pivot * (both + pltpu.roll(both, 1, 1))
        some = diagonal > 0.0
        return jnp.where(some, 1.0 / jnp.where(some, diagonal, 1.0), 0.0)

    def step_of(residual, inverse_diagonal):
        step = (residual * (inverse_diagonal * (1.0 / spectral_mid))[None]).astype(BF16)
        return step.astype(F32).reshape(48, -1)

    def renew(old, step0, residual0, applied, mask, inverse_diagonal):
        width = mask.shape[-1]
        residual = residual0 - applied.reshape(3, DEPTH, width) * mask[None]
        step0 = step0.astype(F32).reshape(3, DEPTH, width)
        step1 = (second * first) * step0 + residual * (
            (2.0 * second / spectral_half) * inverse_diagonal
        )[None]
        new = old.astype(F32).reshape(3, DEPTH, width) + step0 + step1
        return new.astype(BF16).astype(F32).reshape(48, width)

    def first_pair(row, carry):
        before, weight = carry
        applied, after = forces(uu, row, before)
        for i in range(2):
            here = st[row + i] + pltpu.roll(st[row + i], 1, 0)
            inverse_diagonal = invert(here + weight)
            weight = here
            inv[row + i] = inverse_diagonal
            residual = loads[row + i] - applied[i].reshape(3, DEPTH, COLS)
            residual = residual * free[row + i][None]
            res[row + i] = residual
            put(ss, row + i, step_of(residual, inverse_diagonal))
        return after, weight

    zero = jnp.zeros((2, 48, COLS), F32)
    def second_pair(row, carry):
        applied, after = forces(ss, row, carry)
        for i in range(2):
            at = pl.ds((row + i) * 96, 48)
            new = renew(uu[at, :], ss[at, :], res[row + i], applied[i], free[row + i], inv[row + i])
            put(vv, row + i, new)
        return after

    def energy(x):
        f = jnp.dot(matrix[...], x, preferred_element_type=F32).reshape(2, 12, DEPTH, WIDE)
        u = x.astype(F32).reshape(12, DEPTH, WIDE)
        over = jnp.sum(f[1] * u, axis=0)
        return jnp.sum(f[0] * u, axis=0) + pltpu.roll(over, DEPTH - 1, 0)

    def energy_pair(row, carry):
        value = energy(two(vv, row))
        for i in range(2):
            at = row + i - 2
            ratio[at, :, 0:COLS] = value[:, i * COLS : (i + 1) * COLS] * co[at] * inverse[at]
        return carry

    carry, other_carry = (zero, jnp.zeros((DEPTH, COLS), F32)), zero
    for turn in range(LAST):
        if turn < 8:
            carry = first_pair(2 * turn, carry)
        if turn == AT[0]:
            here_b = st_b + pltpu.roll(st_b, 1, 0)
            inv_b = invert(here_b + pltpu.roll(here_b, 16, 1))
            res_b = (loads_b[...] - forces_slots(ub[...]).reshape(3, DEPTH, WIDE)) * free_b[...][None]
            put_slots(sb, step_of(res_b, inv_b), None)
        if 0 <= turn - LAG[0] < 7:
            other_carry = second_pair(2 * (turn - LAG[0]) + 1, other_carry)
        if turn == AT[1]:
            new_b = renew(ub[0:48, :], sb[0:48, :], res_b, forces_slots(sb[...]), free_b[...], inv_b)
            put_slots(vb, new_b, None)
        if 0 <= turn - LAG[1] < 6:
            energy_pair(2 * (turn - LAG[1]) + 2, 0)
        if turn == AT[2]:
            ratio_b = energy(vb[...]) * co_b * inverse_b[...]
    for at in range(12):
        row = at + 2
        part = ratio_b[:, (row // 8) * COLS : (row // 8 + 1) * COLS]
        ratio[at, :, COLS:WIDE] = pltpu.roll(part, (COLS - 16 * (row % 8)) % COLS, 1)

    for y in range(ROWS):
        row, half = y + LOW, (y + LOW) // 8
        part = new_b[:, half * COLS : (half + 1) * COLS]
        part = pltpu.roll(part, (SLOT - 16 * (row % 8)) % COLS, 1)
        own = pltpu.roll(vv[row * 96 : row * 96 + 48, :].astype(F32), COLS - LOW, 1)
        own = jnp.where(iota((48, COLS), 1) <= SEAM, own, part)
        for c in range(3):
            out_f[pl.ds(c * 128 + y, DEPTH, stride=ROWS), :] = own[c * 16 : c * 16 + 16]
    smoothed[...] = out_f[...].astype(BF16)

    for y in range(ROWS):
        a = jnp.concatenate(
            [ratio[y + 2], ratio[y + 1] + ratio[y + 3], ratio[y] + ratio[y + 4]], axis=0
        )
        s = jnp.dot(bands_z[...], a.astype(BF16), preferred_element_type=F32).astype(BF16)
        for k in range(6):
            layers[y * DEPTH : (y + 1) * DEPTH, k * WIDE : (k + 1) * WIDE] = s[
                k * DEPTH : (k + 1) * DEPTH
            ]
    total = jnp.dot(layers[...], bands_x[...], preferred_element_type=F32)
    for y in range(ROWS):
        filtered[pl.ds(y, DEPTH, stride=ROWS), :] = total[y * DEPTH : (y + 1) * DEPTH] * keep[y]


def main_scratch():
    return [
        pltpu.VMEM((17 * 96, COLS), BF16),
        pltpu.VMEM((16 * 96, COLS), BF16),
        pltpu.VMEM((15 * 96, COLS), BF16),
        pltpu.VMEM((192, WIDE), BF16),
        pltpu.VMEM((192, WIDE), BF16),
        pltpu.VMEM((192, WIDE), BF16),
        pltpu.VMEM((16, DEPTH, COLS), F32),
        pltpu.VMEM((12, DEPTH, COLS), F32),
        pltpu.VMEM((16, 3, DEPTH, COLS), F32),
        pltpu.VMEM((16, DEPTH, COLS), F32),
        pltpu.VMEM((12, DEPTH, WIDE), F32),
        pltpu.VMEM((128, 6 * WIDE), BF16),
        pltpu.VMEM((384, 128), F32),
    ]


def swapped(shard, axis, odd):
    size = lax.axis_size(axis)
    partner = [((i - odd) ^ 1) + odd for i in range(size)]
    return lax.ppermute(shard, axis, [(i, j) for i, j in enumerate(partner) if 0 <= j < size])


def shards(displacement, density, solid, fixed_nodes, load_nodes, load_forces):
    grid_y = ROWS * lax.axis_size("gy")
    grid_x = COLS * lax.axis_size("gx")
    table = stiffness_table()
    pivot = float(table[0, 0])
    tile = (DEPTH, COLS)

    given = (
        displacement.reshape(384, 128),
        density.reshape(128, 128),
        solid.reshape(128, 128),
        load_nodes.reshape(1, -1),
    )
    um, st, co, keep, own, far, near, inverse, inverse_b, nodes = call(
        lambda *refs: pack_body(grid_y, grid_x, *refs),
        [
            shape_of((ROWS, 3) + tile, BF16),
            shape_of((ROWS,) + tile, F32),
            shape_of((ROWS,) + tile, F32),
            shape_of((ROWS,) + tile, F32),
            shape_of((5,) + tile, BF16),
            shape_of((5,) + tile, BF16),
            shape_of((5,) + tile, BF16),
            shape_of((12,) + tile, F32),
            shape_of((DEPTH, WIDE), F32),
            shape_of((1, load_nodes.shape[0]), I32),
        ],
        [pltpu.with_memory_space_constraint(array, pltpu.HBM) for array in given],
        [
            pltpu.VMEM((384, 128), BF16),
            pltpu.VMEM((128, 128), F32),
            pltpu.VMEM((128, 128), I32),
            pltpu.VMEM((384, 128), F32),
            pltpu.SemaphoreType.DMA((4,)),
        ],
        space=pltpu.HBM,
    )
    st, _ = lax.optimization_barrier((st, near))
    from_far = swapped(far, "gx", 1)
    from_near = swapped(near, "gx", 0)
    *loads, um, st, co = call(
        lambda *refs: load_body(grid_y, grid_x, *refs),
        [
            shape_of((16, 3) + tile, F32),
            shape_of((3, DEPTH, WIDE), F32),
            shape_of((ROWS, 5) + tile, BF16),
            shape_of((ROWS,) + tile, F32),
            shape_of((ROWS,) + tile, F32),
        ],
        [nodes, load_forces.T, um, st, co],
        flops=1000000000,
    )
    from_far, from_near, um = lax.optimization_barrier((from_far, from_near, um))
    far, near, tiles, st, co, slots = call(
        merge_body,
        [
            shape_of((26,) + tile, BF16),
            shape_of((26,) + tile, BF16),
            shape_of((ROWS, 5) + tile, BF16),
            shape_of((ROWS,) + tile, F32),
            shape_of((ROWS,) + tile, F32),
            shape_of((5,) + tile, BF16),
        ],
        [um, st, co, own, from_far, from_near],
    )
    fixed, _ = lax.optimization_barrier((fixed_nodes, near))
    from_far = swapped(far, "gy", 1)
    from_near = swapped(near, "gy", 0)
    free, free_b = call(
        lambda *refs: mask_body(grid_y, grid_x, *refs),
        [
            shape_of((16,) + tile, F32),
            shape_of((DEPTH, WIDE), F32),
        ],
        [fixed.reshape(1, -1)],
        [pltpu.VMEM((256, WIDE), F32)],
        flops=1000000000,
    )
    smoothed, filtered = call(
        lambda *refs: main_body(pivot, *refs),
        [shape_of((384, 128), BF16), shape_of((128, 128), F32)],
        [
            tiles,
            st,
            co,
            slots,
            keep,
            from_far,
            from_near,
            free,
            free_b,
            *loads,
            inverse,
            inverse_b,
            jnp.asarray(element_matrix(table), BF16),
            jnp.asarray(depth_bands(), BF16),
            jnp.asarray(along_bands(), BF16),
        ],
        main_scratch(),
        flops=10000000000,
    )
    return smoothed.reshape(3, DEPTH, ROWS, COLS), filtered.reshape(DEPTH, ROWS, COLS)


def solution(mesh):
    placed = (P(None, None, "gy", "gx"), P(None, "gy", "gx"), P(None, "gy", "gx"), P(), P(), P())
    return jax.shard_map(
        shards,
        mesh=mesh,
        in_specs=placed,
        out_specs=(P(None, None, "gy", "gx"), P(None, "gy", "gx")),
        check_vma=False,
    )
```
